32 devices in a mesh: groups: 2 (over x), dp: 16 (over z, y, core).
Axes of the slice: x: 2, y: 2, z: 4, core: 2. Of those that a mesh axis runs over, the one named last changes fastest.
Arguments:
- teacher_hidden: bfloat16 [256, 4096], P(('groups', 'dp')), parts along dimension 0, may hold values from -128 to 128
- student_hidden: bfloat16 [256, 4096], P(('groups', 'dp')), parts along dimension 0, may hold values from -128 to 128
- teacher_head: bfloat16 [4096, 8192], P(None, 'dp'), may hold values from -0.09375 to 0.09375
- student_head: bfloat16 [4096, 8192], P(None, 'dp'), may hold values from -0.09375 to 0.09375
- labels: int32 [256], P('groups'), parts along dimension 0, may hold values from 0 to 8191
- order: int32 [256], P('groups'), parts along dimension 0, may hold values from 0 to 127, each once
Outputs:
- row_loss: float32 [256], P(('groups', 'dp')), parts along dimension 0
- grad_hidden: float32 [256, 4096], P(('groups', 'dp')), parts along dimension 0
- grad_head: bfloat16 [8192, 8192], P('groups', 'dp'), parts along dimension 0
The draws below stay inside these ranges and needn't reach their ends.
There are 2 independent parts, one for each index of `groups`. The reference program is written for one: setup_inputs(seed, part) draws one part's arguments, and reference() takes and returns one part's arrays. A program takes and returns all parts, laid end to end along the dimension named above; an argument that names none is the same for every part. Nothing has to cross between parts.
Inputs may be any that keep to these rules, and one draw needn't show every extreme that they name: `order`: a permutation of the rows.
All inputs are finite; a program needn't handle non-finite values.
Results may differ from the reference program's by a relative error of at most 0.0044.
Values may be sent and summed in bfloat16 or wider, within the bound.
No kernel may reach another device: no remote copies, remote signals or barrier semaphores. Data moves between devices by JAX's collectives and lax.ppermute only.
A program may use at most 128 MiB of HBM per device.

```python
import math
import jax
import jax.numpy as jnp
import numpy as np
from jax import lax

DT = 4096
DS = 4096
TOKENS = 128
VOCAB = 8192


def draw_teacher_hidden(key, part):
    key = jax.random.fold_in(key, 7)
    spread_key, base_key = jax.random.split(key, 2)
    spread = jnp.exp(jax.random.uniform(spread_key, (TOKENS, 1), jnp.float32, math.log(2.0), math.log(12.0)))
    base = jnp.clip(jax.random.normal(base_key, (TOKENS, DT), jnp.float32), -4.0, 4.0)
    rows = base * spread
    return rows.astype(jnp.bfloat16)


def draw_student_hidden(key, part):
    key = jax.random.fold_in(key, 13)
    spread_key, base_key = jax.random.split(key, 2)
    spread = jnp.exp(jax.random.uniform(spread_key, (TOKENS, 1), jnp.float32, math.log(2.0), math.log(12.0)))
    base = jnp.clip(jax.random.normal(base_key, (TOKENS, DS), jnp.float32), -4.0, 4.0)
    rows = base * spread
    return rows.astype(jnp.bfloat16)


def touch_ends(drawn, stream_key, low, largest):
    place = [jax.random.randint(jax.random.fold_in(stream_key, axis), (), 0, length) for axis, length in enumerate(drawn.shape)]
    main_axis = drawn.shape.index(max(drawn.shape))
    next_to = place[:main_axis] + [(place[main_axis] + 1) % drawn.shape[main_axis]] + place[main_axis + 1:]
    return drawn.at[tuple(place)].set(low).at[tuple(next_to)].set(largest)


def block_scale(stream_key, dims, cuts, low, largest):
    gain = 1.0
    for dim, shards_of in cuts:
        heights = jax.random.uniform(jax.random.fold_in(jax.random.fold_in(stream_key, 6), dim), (shards_of,), jnp.float32, low / len(cuts), largest / len(cuts))
        gain = gain * jnp.repeat(jnp.exp(heights), dims[dim] // shards_of).reshape((-1,) + (1,) * (len(dims) - 1 - dim))
    return gain


def rank_table(count, skew):
    weights = [(1 << 20) // math.isqrt(grade ** skew) + 1 for grade in range(1, count + 1)]
    scale = 1 + sum(weights) // (1 << 30)
    return np.cumsum(np.array([max(1, weight // scale) for weight in weights]))


def ranked(rng, dims, amount, slope):
    listing = rank_table(amount, slope)
    ticket = jax.random.randint(jax.random.fold_in(rng, 1), dims, 0, int(listing[amount - 1]))
    standing = jnp.searchsorted(jnp.asarray(listing, jnp.int32), ticket, side="right")
    return jax.random.permutation(jax.random.fold_in(rng, 2), amount)[standing].astype(jnp.int32)


def bell_draw(own_key, extent, width, limit, shards=(), held_as=jnp.bfloat16):
    result = jax.random.normal(own_key, extent, jnp.float32) * width
    if len(shards) > 0:
        result = block_scale(own_key, extent, shards, -0.22, 0.18) * result
    return jnp.clip(result, min=-limit, max=limit).astype(held_as)


def setup_inputs(seed: int = 0, part: int = 0) -> dict:
    seeds = jax.random.split(jax.random.key(seed), 7)
    part_splits = jax.random.split(jax.random.fold_in(seeds[6], part), 7)
    return {
        "teacher_hidden": draw_teacher_hidden(jax.random.fold_in(jax.random.fold_in(seeds[6], part), 71), part),
        "student_hidden": draw_student_hidden(jax.random.fold_in(jax.random.fold_in(seeds[6], part), 71), part),
        "teacher_head": bell_draw(seeds[2], (DT, VOCAB), DT ** -0.5, 0.09375, ((1, 16),)),
        "student_head": bell_draw(seeds[3], (DS, VOCAB), DS ** -0.5, 0.09375, ((1, 16),)),
        "labels": touch_ends(ranked(part_splits[4], (TOKENS,), VOCAB, 2), jax.random.fold_in(part_splits[4], 3), 0, VOCAB - 1).astype(jnp.int32),
        "order": jax.random.permutation(part_splits[5], TOKENS).astype(jnp.int32),
    }


CE_WEIGHT = 0.5


def reference(teacher_hidden, student_hidden, teacher_head, student_head, labels, order):
    paired = jnp.take(teacher_hidden, order.astype(jnp.int32), axis=0)
    teacher_logits = jnp.dot(paired, teacher_head, preferred_element_type=jnp.float32)
    student_logits = jnp.dot(student_hidden, student_head, preferred_element_type=jnp.float32)
    teacher_max = jnp.max(teacher_logits, axis=1)
    student_max = jnp.max(student_logits, axis=1)
    teacher_exp = jnp.exp(teacher_logits - teacher_max[:, None])
    student_exp = jnp.exp(student_logits - student_max[:, None])
    teacher_total = jnp.sum(teacher_exp, axis=1)
    student_total = jnp.sum(student_exp, axis=1)
    cross = jnp.sum(teacher_exp * (teacher_logits - student_logits), axis=1)
    columns = lax.iota(jnp.int32, VOCAB)
    is_label = labels.astype(jnp.int32)[:, None] == columns[None, :]
    label_logit = jnp.sum(jnp.where(is_label, student_logits, jnp.zeros_like(student_logits)), axis=1)
    teacher_norm = teacher_max + jnp.log(teacher_total)
    student_norm = student_max + jnp.log(student_total)
    row_loss = cross / teacher_total - teacher_norm + student_norm + CE_WEIGHT * (student_norm - label_logit)
    onehot = jnp.where(is_label, 1.0, 0.0).astype(student_logits.dtype)
    logit_grad = ((1.0 + CE_WEIGHT) * jnp.exp(student_logits - student_norm[:, None])
                  - jnp.exp(teacher_logits - teacher_norm[:, None]) - CE_WEIGHT * onehot).astype(jnp.bfloat16)
    grad_head = lax.dot_general(student_hidden, logit_grad, (((0,), (0,)), ((), ())),
                                preferred_element_type=jnp.float32).astype(jnp.bfloat16)
    grad_hidden = lax.dot_general(logit_grad, student_head, (((1,), (1,)), ((), ())),
                                  preferred_element_type=jnp.float32)
    return (row_loss, grad_hidden, grad_head)
```

```python
import functools

import jax
import jax.numpy as jnp
from jax import lax
from jax.experimental import pallas as pl
from jax.experimental.pallas import tpu as pltpu
from jax.sharding import PartitionSpec as P

CE_WEIGHT = 0.5
STATS = 8


def xor_order(n):
    return (0, 4, 2, 6, 8, 12, 10, 14, 1, 5, 3, 7, 9, 13, 11, 15) if n == 16 else None


def held_rows(shape, dim, me, rows_local, tuned):
    held = lax.broadcasted_iota(jnp.int32, shape, dim)
    if not tuned:
        return held
    step = rows_local.bit_length() - 1
    block = lax.shift_right_logical(held, step)
    bit = lambda k: lax.shift_right_logical(block, k) & 1
    distance = bit(3) + bit(2) * 8 + bit(1) * 2 + bit(0) * 4
    return (me ^ distance) * rows_local + (held & (rows_local - 1))


def to_column(is_row, row):
    return jnp.sum(jnp.where(is_row, row, 0.0), axis=1, keepdims=True)


def logits_kernel(rows_local, tuned, parts, me_ref, order_ref, labels_ref, *refs):
    teacher_rows, student_rows = refs[:parts], refs[parts : 2 * parts]
    teacher_head, student_head, teacher_out, student_out, stats_out, teacher_acc, student_acc = refs[2 * parts :]
    step = pl.program_id(0)

    @pl.when(step == 0)
    def _():
        teacher_acc[...] = jnp.zeros_like(teacher_acc)
        student_acc[...] = jnp.zeros_like(student_acc)

    def rows(pieces):
        return jnp.concatenate([piece[...] for piece in pieces], axis=0)

    teacher_acc[...] += jnp.dot(rows(teacher_rows), teacher_head[...], preferred_element_type=jnp.float32)
    student_acc[...] += jnp.dot(rows(student_rows), student_head[...], preferred_element_type=jnp.float32)

    @pl.when(step == pl.num_programs(0) - 1)
    def _():
        me = me_ref[0]
        count, vocab = student_acc.shape
        lanes = lax.broadcasted_iota(jnp.int32, (count, count), 1)
        is_row = held_rows((count, count), 0, me, rows_local, tuned) == lanes
        wanted = to_column(is_row, order_ref[...].astype(jnp.float32))
        have = held_rows((count, count), 1, me, rows_local, tuned).astype(jnp.float32)
        pick = jnp.where(wanted == have, 1.0, 0.0).astype(jnp.bfloat16)
        raw = teacher_acc[...]
        high = raw.astype(jnp.bfloat16)
        rest = raw - high.astype(jnp.float32)
        middle = rest.astype(jnp.bfloat16)
        low = (rest - middle.astype(jnp.float32)).astype(jnp.bfloat16)
        teacher = sum(jnp.dot(pick, piece, preferred_element_type=jnp.float32) for piece in (high, middle, low))
        student = student_acc[...]
        teacher_out[...] = teacher
        student_out[...] = student
        label = to_column(is_row, labels_ref[...].astype(jnp.float32)).astype(jnp.int32)
        is_label = label == lax.broadcasted_iota(jnp.int32, (count, vocab), 1) + me * vocab
        teacher_max = jnp.max(teacher, axis=1, keepdims=True)
        student_max = jnp.max(student, axis=1, keepdims=True)
        teacher_exp = jnp.exp(teacher - teacher_max)
        values = (
            teacher_max,
            student_max,
            jnp.sum(teacher_exp, axis=1, keepdims=True),
            jnp.sum(jnp.exp(student - student_max), axis=1, keepdims=True),
            jnp.sum(teacher_exp * (teacher - student), axis=1, keepdims=True),
            jnp.sum(jnp.where(is_label, student, 0.0), axis=1, keepdims=True),
        )
        block = [jnp.sum(jnp.where(is_row, value, 0.0), axis=0, keepdims=True) for value in values]
        block.append(jnp.zeros((STATS - len(block), count), jnp.float32))
        stats_out[...] = jnp.broadcast_to(jnp.concatenate(block, axis=0)[None], stats_out.shape)


def logits(me, order, labels, hidden, heads, n, rows_local, tuned):
    count = sum(piece.shape[0] for piece in hidden)
    depth, vocab = heads[0].shape
    step = min(512, depth)
    steps = depth // step

    def columns(piece, first):
        return pl.BlockSpec((piece.shape[0], step), lambda k: (0, k + first))

    whole = lambda shape: pl.BlockSpec(shape, lambda k: (0,) * len(shape))
    return pl.pallas_call(
        functools.partial(logits_kernel, rows_local, tuned, len(hidden)),
        grid=(steps,),
        in_specs=[pl.BlockSpec(memory_space=pltpu.SMEM), whole((1, count)), whole((1, count))]
        + [columns(piece, 0) for piece in hidden]
        + [columns(piece, steps) for piece in hidden]
        + [pl.BlockSpec((step, vocab), lambda k: (k, 0))] * 2,
        out_specs=(whole((count, vocab)), whole((count, vocab)), whole((n, STATS, count))),
        out_shape=(
            jax.ShapeDtypeStruct((count, vocab), jnp.float32),
            jax.ShapeDtypeStruct((count, vocab), jnp.float32),
            jax.ShapeDtypeStruct((n, STATS, count), jnp.float32),
        ),
        scratch_shapes=[pltpu.VMEM((count, vocab), jnp.float32)] * 2,
        compiler_params=pltpu.CompilerParams(vmem_limit_bytes=40 * 2**20),
        cost_estimate=pl.CostEstimate(
            flops=4 * count * depth * vocab, bytes_accessed=4 * depth * (vocab + count), transcendentals=2 * count * vocab
        ),
    )(me, order[None], labels[None], *hidden, *hidden, *heads)


def grad_kernel(
    rows_local, tuned, me_ref, labels_ref, stats_ref, teacher_ref, student_ref, head_ref, keep_out, send_out, grad_out, loss_out
):
    @pl.when(pl.program_id(0) == 0)
    def _():
        me = me_ref[0]
        count, vocab = student_ref.shape
        devices = stats_ref.shape[0]
        top = stats_ref[0, 0:2]
        for d in range(1, devices):
            top = jnp.maximum(top, stats_ref[d, 0:2])
        totals = jnp.zeros((2, count), jnp.float32)
        cross = jnp.zeros((1, count), jnp.float32)
        label_logit = jnp.zeros((1, count), jnp.float32)
        for d in range(devices):
            weight = jnp.exp(stats_ref[d, 0:2] - top)
            totals += weight * stats_ref[d, 2:4]
            cross += weight[0:1] * stats_ref[d, 4:5]
            label_logit += stats_ref[d, 5:6]
        norms = top + jnp.log(totals)
        teacher_norm, student_norm = norms[0:1], norms[1:2]
        loss = cross / totals[0:1] - teacher_norm + student_norm + CE_WEIGHT * (student_norm - label_logit)
        lanes = lax.broadcasted_iota(jnp.int32, (count, count), 1)
        is_row = held_rows((count, count), 0, me, rows_local, tuned) == lanes
        mine = lax.broadcasted_iota(jnp.int32, (count, count), 0) + me * rows_local == lanes
        by_lane = lax.broadcasted_iota(jnp.int32, (count, count), 0) == lanes
        loss_out[...] = jnp.sum(jnp.where(by_lane, to_column(mine, loss), 0.0), axis=0, keepdims=True)
        label = to_column(is_row, labels_ref[...].astype(jnp.float32)).astype(jnp.int32)
        is_label = label == lax.broadcasted_iota(jnp.int32, (count, vocab), 1) + me * vocab
        grad_out[...] = (
            (1.0 + CE_WEIGHT) * jnp.exp(student_ref[...] - to_column(is_row, student_norm))
            - jnp.exp(teacher_ref[...] - to_column(is_row, teacher_norm))
            - jnp.where(is_label, CE_WEIGHT, 0.0)
        ).astype(jnp.bfloat16)

    part = lax.dot_general(
        grad_out[...], head_ref[...], (((1,), (1,)), ((), ())), preferred_element_type=jnp.float32
    )
    kept = keep_out.shape[0]
    keep_out[...] = part[:kept]
    if send_out is not None:
        send_out[...] = part[kept:].astype(jnp.bfloat16)


def gradient(me, labels, stats, teacher_logits, student_logits, head, rows_local, tuned):
    count, vocab = student_logits.shape
    depth = head.shape[0]
    step = min(512, depth)
    kept = count // 2 if tuned else count
    whole = lambda shape: pl.BlockSpec(shape, lambda k: (0,) * len(shape))
    column = lambda rows: pl.BlockSpec((rows, step), lambda k: (0, k))
    shapes = [jax.ShapeDtypeStruct((kept, depth), jnp.float32)]
    specs = [column(kept)]
    if tuned:
        shapes.append(jax.ShapeDtypeStruct((count - kept, depth), jnp.bfloat16))
        specs.append(column(count - kept))
    shapes += [jax.ShapeDtypeStruct((count, vocab), jnp.bfloat16), jax.ShapeDtypeStruct((1, count), jnp.float32)]
    specs += [whole((count, vocab)), whole((1, count))]

    def kernel(*refs):
        if tuned:
            grad_kernel(rows_local, tuned, *refs)
        else:
            grad_kernel(rows_local, tuned, *refs[:7], None, *refs[7:])

    return pl.pallas_call(
        kernel,
        grid=(depth // step,),
        in_specs=[
            pl.BlockSpec(memory_space=pltpu.SMEM),
            whole((1, count)),
            whole(stats.shape),
            whole((count, vocab)),
            whole((count, vocab)),
            pl.BlockSpec((step, vocab), lambda k: (k, 0)),
        ],
        out_specs=tuple(specs),
        out_shape=tuple(shapes),
        compiler_params=pltpu.CompilerParams(vmem_limit_bytes=40 * 2**20),
        cost_estimate=pl.CostEstimate(
            flops=2 * count * depth * vocab, bytes_accessed=2 * depth * (vocab + 2 * count), transcendentals=2 * count * vocab
        ),
    )(me, labels[None], stats, teacher_logits, student_logits, head)


def head_kernel(parts, *refs):
    rows = jnp.concatenate([piece[...] for piece in refs[:parts]], axis=0)
    grad_ref, out_ref = refs[parts:]
    out_ref[...] = lax.dot_general(
        rows, grad_ref[...], (((0,), (0,)), ((), ())), preferred_element_type=jnp.float32
    ).astype(jnp.bfloat16)


def head_gradient(hidden, logit_grad, depth):
    count, vocab = logit_grad.shape
    step = min(512, depth)
    first = depth // step
    return pl.pallas_call(
        functools.partial(head_kernel, len(hidden)),
        grid=(depth // step,),
        in_specs=[pl.BlockSpec((piece.shape[0], step), lambda k: (0, k + first)) for piece in hidden]
        + [pl.BlockSpec((count, vocab), lambda k: (0, 0))],
        out_specs=pl.BlockSpec((step, vocab), lambda k: (k, 0)),
        out_shape=jax.ShapeDtypeStruct((depth, vocab), jnp.bfloat16),
        compiler_params=pltpu.CompilerParams(vmem_limit_bytes=40 * 2**20),
        cost_estimate=pl.CostEstimate(
            flops=2 * count * depth * vocab, bytes_accessed=2 * depth * (vocab + count), transcendentals=0
        ),
    )(*hidden, logit_grad)


def swap(value, distance, n):
    return lax.ppermute(value, "dp", [(i, i ^ distance) for i in range(n)])


def gather_rows(rows, n):
    far = swap(rows, 8, n)
    side = swap(rows, 2, n)
    near = swap(rows, 4, n)
    far_near = swap(far, 4, n)
    near_side = swap(near, 2, n)
    far_side = swap(far, 2, n)
    far_near_side = swap(far_near, 2, n)
    first = jnp.concatenate([rows, near, side, near_side], axis=0)
    second = jnp.concatenate([far, far_near, far_side, far_near_side], axis=0)
    return [first, second, swap(first, 1, n), swap(second, 1, n)]


def scatter_rows(keep, send, rows_local, n):
    low = jnp.bfloat16
    full = jnp.float32
    held = keep + swap(send, 1, n).astype(full)
    quarter = 2 * rows_local
    near_keep, near_send, far_keep, far_send = (held[k * quarter : (k + 1) * quarter] for k in range(4))
    far = (far_keep + swap(far_send.astype(low), 2, n).astype(full)).astype(low)
    near = near_keep + swap(near_send.astype(low), 2, n).astype(full)
    from_far = swap(far[:rows_local], 8, n)
    from_far_near = swap(far[rows_local:], 12, n)
    from_near = swap(near[rows_local:].astype(low), 4, n)
    return near[:rows_local] + from_far.astype(full) + from_far_near.astype(full) + from_near.astype(full)


def per_device(n, teacher_hidden, student_hidden, teacher_head, student_head, labels, order):
    rows_local, depth = student_hidden.shape
    tuned = xor_order(n) is not None and rows_local == 8
    me = lax.axis_index("dp").astype(jnp.int32).reshape(1)
    rows = jnp.concatenate([teacher_hidden, student_hidden], axis=1)
    hidden = gather_rows(rows, n) if tuned else [lax.all_gather(rows, "dp", axis=0, tiled=True)]
    teacher_logits, student_logits, stats = logits(
        me, order, labels, hidden, (teacher_head, student_head), n, rows_local, tuned
    )
    stats = lax.all_to_all(stats, "dp", 0, 0)
    outs = gradient(me, labels, stats, teacher_logits, student_logits, student_head, rows_local, tuned)
    logit_grad, loss = outs[-2:]
    grad_head = head_gradient(hidden, logit_grad, depth)
    if tuned:
        grad_hidden = scatter_rows(outs[0], outs[1], rows_local, n)
    else:
        grad_hidden = lax.psum_scatter(outs[0], "dp", scatter_dimension=0, tiled=True)
    return (loss[0, :rows_local], grad_hidden, grad_head)


def solution(mesh):
    in_specs = (
        P(("groups", "dp"), None),
        P(("groups", "dp"), None),
        P(None, "dp"),
        P(None, "dp"),
        P("groups"),
        P("groups"),
    )
    out_specs = (P(("groups", "dp")), P(("groups", "dp"), None), P("groups", "dp"))
    return jax.shard_map(
        functools.partial(per_device, mesh.shape["dp"]),
        mesh=mesh,
        in_specs=in_specs,
        out_specs=out_specs,
        check_vma=False,
    )
```

```python
import functools

import jax
import jax.numpy as jnp
from jax import lax
from jax.experimental import pallas as pl
from jax.experimental.pallas import tpu as pltpu
from jax.sharding import PartitionSpec as P

CE_WEIGHT = 0.5
STATS = 8


def xor_order(n):
    return (0, 4, 2, 6, 8, 12, 10, 14, 1, 5, 3, 7, 9, 13, 11, 15) if n == 16 else None


def held_rows(shape, dim, me, rows_local, tuned):
    held = lax.broadcasted_iota(jnp.int32, shape, dim)
    if not tuned:
        return held
    step = rows_local.bit_length() - 1
    block = lax.shift_right_logical(held, step)
    bit = lambda k: lax.shift_right_logical(block, k) & 1
    distance = bit(3) + bit(2) * 8 + bit(1) * 2 + bit(0) * 4
    return (me ^ distance) * rows_local + (held & (rows_local - 1))


def to_column(is_row, row):
    return jnp.sum(jnp.where(is_row, row, 0.0), axis=1, keepdims=True)


def prepare_kernel(
    rows_local, tuned, me_ref, order_ref, labels_ref, teacher_ref, student_ref, teacher_out, student_out, pick_out, label_out, sems
):
    copies = []
    pieces = sems.shape[1]
    rows = teacher_ref.shape[0] // pieces
    for k in range(pieces):
        for j, (source, target) in enumerate(((teacher_ref, teacher_out), (student_ref, student_out))):
            part = pl.ds(k * rows, rows)
            copies.append(pltpu.make_async_copy(source.at[part], target.at[part], sems.at[j, k]))
    for copy in copies:
        copy.start()
    me = me_ref[0]
    count = order_ref.shape[1]
    vocab = teacher_ref.shape[1]
    lanes = lax.broadcasted_iota(jnp.int32, (count, count), 1)
    is_row = held_rows((count, count), 0, me, rows_local, tuned) == lanes
    wanted = to_column(is_row, order_ref[...].astype(jnp.float32))
    have = held_rows((count, count), 1, me, rows_local, tuned).astype(jnp.float32)
    pick_out[...] = jnp.where(wanted == have, 1.0, 0.0).astype(jnp.bfloat16)
    label = to_column(is_row, labels_ref[...].astype(jnp.float32)) - (me * vocab).astype(jnp.float32)
    label_out[...] = jnp.broadcast_to(label, label_out.shape)
    for copy in copies:
        copy.wait()


def prepare(me, order, labels, heads, rows_local, tuned):
    count = order.shape[0]
    vmem = pl.BlockSpec(memory_space=pltpu.VMEM)
    hbm = pl.BlockSpec(memory_space=pltpu.HBM)
    return pl.pallas_call(
        functools.partial(prepare_kernel, rows_local, tuned),
        in_specs=[pl.BlockSpec(memory_space=pltpu.SMEM), vmem, vmem, hbm, hbm],
        out_specs=(vmem,) * 4,
        out_shape=(
            jax.ShapeDtypeStruct(heads[0].shape, heads[0].dtype),
            jax.ShapeDtypeStruct(heads[1].shape, heads[1].dtype),
            jax.ShapeDtypeStruct((count, count), jnp.bfloat16),
            jax.ShapeDtypeStruct((count, 128), jnp.float32),
        ),
        scratch_shapes=[pltpu.SemaphoreType.DMA((2, 4))],
        compiler_params=pltpu.CompilerParams(vmem_limit_bytes=24 * 2**20),
        cost_estimate=pl.CostEstimate(flops=0, bytes_accessed=2 * heads[0].size * 4, transcendentals=0),
    )(me, order[None], labels[None], *(pltpu.with_memory_space_constraint(head, pltpu.HBM) for head in heads))


def logits_kernel(rows_local, tuned, parts, me_ref, pick_ref, label_ref, *refs):
    pieces = refs[:parts]
    teacher_head, student_head, teacher_out, student_out, stats_out = refs[parts:]
    depth, vocab = student_head.shape

    def product(first, head):
        rows = jnp.concatenate([piece[:, first : first + depth] for piece in pieces], axis=0)
        return jnp.dot(rows, head[...], preferred_element_type=jnp.float32)

    me = me_ref[0]
    raw = product(0, teacher_head)
    student = product(depth, student_head)
    count = student.shape[0]
    high = raw.astype(jnp.bfloat16)
    rest = raw - high.astype(jnp.float32)
    middle = rest.astype(jnp.bfloat16)
    low = (rest - middle.astype(jnp.float32)).astype(jnp.bfloat16)
    pick = pick_ref[...]
    teacher = sum(jnp.dot(pick, piece, preferred_element_type=jnp.float32) for piece in (high, middle, low))
    teacher_out[...] = teacher
    student_out[...] = student
    is_label = label_ref[:, 0:1].astype(jnp.int32) == lax.broadcasted_iota(jnp.int32, (count, vocab), 1)
    teacher_max = jnp.max(teacher, axis=1, keepdims=True)
    student_max = jnp.max(student, axis=1, keepdims=True)
    teacher_exp = jnp.exp(teacher - teacher_max)
    values = (
        teacher_max,
        student_max,
        jnp.sum(teacher_exp, axis=1, keepdims=True),
        jnp.sum(jnp.exp(student - student_max), axis=1, keepdims=True),
        jnp.sum(teacher_exp * (teacher - student), axis=1, keepdims=True),
        jnp.sum(jnp.where(is_label, student, 0.0), axis=1, keepdims=True),
    )
    lanes = lax.broadcasted_iota(jnp.int32, (count, count), 1)
    is_row = held_rows((count, count), 0, me, rows_local, tuned) == lanes
    block = [jnp.sum(jnp.where(is_row, value, 0.0), axis=0, keepdims=True) for value in values]
    block.append(jnp.zeros((STATS - len(block), count), jnp.float32))
    stats_out[...] = jnp.broadcast_to(jnp.concatenate(block, axis=0)[None], stats_out.shape)


def logits(me, pick, label, hidden, heads, n, rows_local, tuned):
    count = pick.shape[0]
    depth, vocab = heads[0].shape
    vmem = pl.BlockSpec(memory_space=pltpu.VMEM)
    return pl.pallas_call(
        functools.partial(logits_kernel, rows_local, tuned, len(hidden)),
        in_specs=[pl.BlockSpec(memory_space=pltpu.SMEM)] + [vmem] * (4 + len(hidden)),
        out_specs=(vmem,) * 3,
        out_shape=(
            jax.ShapeDtypeStruct((count, vocab), jnp.float32),
            jax.ShapeDtypeStruct((count, vocab), jnp.float32),
            jax.ShapeDtypeStruct((n, STATS, count), jnp.float32),
        ),
        compiler_params=pltpu.CompilerParams(vmem_limit_bytes=40 * 2**20),
        cost_estimate=pl.CostEstimate(
            flops=4 * count * depth * vocab, bytes_accessed=4 * depth * (vocab + count), transcendentals=2 * count * vocab
        ),
    )(me, pick, label, *hidden, *heads)


def grad_kernel(
    rows_local, tuned, me_ref, label_ref, stats_ref, teacher_ref, student_ref, head_ref, keep_out, send_out, grad_out, loss_out
):
    me = me_ref[0]
    count, vocab = student_ref.shape
    devices = stats_ref.shape[0]
    top = stats_ref[0, 0:2]
    for d in range(1, devices):
        top = jnp.maximum(top, stats_ref[d, 0:2])
    totals = jnp.zeros((2, count), jnp.float32)
    cross = jnp.zeros((1, count), jnp.float32)
    label_logit = jnp.zeros((1, count), jnp.float32)
    for d in range(devices):
        weight = jnp.exp(stats_ref[d, 0:2] - top)
        totals += weight * stats_ref[d, 2:4]
        cross += weight[0:1] * stats_ref[d, 4:5]
        label_logit += stats_ref[d, 5:6]
    norms = top + jnp.log(totals)
    teacher_norm, student_norm = norms[0:1], norms[1:2]
    loss = cross / totals[0:1] - teacher_norm + student_norm + CE_WEIGHT * (student_norm - label_logit)
    lanes = lax.broadcasted_iota(jnp.int32, (count, count), 1)
    is_row = held_rows((count, count), 0, me, rows_local, tuned) == lanes
    mine = lax.broadcasted_iota(jnp.int32, (count, count), 0) + me * rows_local == lanes
    by_lane = lax.broadcasted_iota(jnp.int32, (count, count), 0) == lanes
    loss_out[...] = jnp.sum(jnp.where(by_lane, to_column(mine, loss), 0.0), axis=0, keepdims=True)
    is_label = label_ref[:, 0:1].astype(jnp.int32) == lax.broadcasted_iota(jnp.int32, (count, vocab), 1)
    grad = (
        (1.0 + CE_WEIGHT) * jnp.exp(student_ref[...] - to_column(is_row, student_norm))
        - jnp.exp(teacher_ref[...] - to_column(is_row, teacher_norm))
        - jnp.where(is_label, CE_WEIGHT, 0.0)
    ).astype(jnp.bfloat16)
    grad_out[...] = grad
    kept = keep_out.shape[0]
    depth = head_ref.shape[0]
    step = min(512, depth)
    for k in range(0, depth, step):
        part = lax.dot_general(
            grad, head_ref[k : k + step], (((1,), (1,)), ((), ())), preferred_element_type=jnp.float32
        )
        keep_out[:, k : k + step] = part[:kept]
        if send_out is not None:
            send_out[:, k : k + step] = part[kept:].astype(jnp.bfloat16)


def gradient(me, label, stats, teacher_logits, student_logits, head, rows_local, tuned):
    count, vocab = student_logits.shape
    depth = head.shape[0]
    kept = count // 2 if tuned else count
    vmem = pl.BlockSpec(memory_space=pltpu.VMEM)
    shapes = [jax.ShapeDtypeStruct((kept, depth), jnp.float32)]
    if tuned:
        shapes.append(jax.ShapeDtypeStruct((count - kept, depth), jnp.bfloat16))
    shapes += [jax.ShapeDtypeStruct((count, vocab), jnp.bfloat16), jax.ShapeDtypeStruct((1, count), jnp.float32)]

    def kernel(*refs):
        if tuned:
            grad_kernel(rows_local, tuned, *refs)
        else:
            grad_kernel(rows_local, tuned, *refs[:7], None, *refs[7:])

    return pl.pallas_call(
        kernel,
        in_specs=[pl.BlockSpec(memory_space=pltpu.SMEM)] + [vmem] * 5,
        out_specs=(vmem,) * len(shapes),
        out_shape=tuple(shapes),
        compiler_params=pltpu.CompilerParams(vmem_limit_bytes=40 * 2**20),
        cost_estimate=pl.CostEstimate(
            flops=2 * count * depth * vocab, bytes_accessed=2 * depth * (vocab + 2 * count), transcendentals=2 * count * vocab
        ),
    )(me, label, stats, teacher_logits, student_logits, head)


def head_kernel(parts, *refs):
    rows = jnp.concatenate([piece[...] for piece in refs[:parts]], axis=0)
    grad_ref, out_ref = refs[parts:]
    out_ref[...] = lax.dot_general(
        rows, grad_ref[...], (((0,), (0,)), ((), ())), preferred_element_type=jnp.float32
    ).astype(jnp.bfloat16)


def head_gradient(hidden, logit_grad, depth):
    count, vocab = logit_grad.shape
    step = min(512, depth)
    first = depth // step
    return pl.pallas_call(
        functools.partial(head_kernel, len(hidden)),
        grid=(depth // step,),
        in_specs=[pl.BlockSpec((piece.shape[0], step), lambda k: (0, k + first)) for piece in hidden]
        + [pl.BlockSpec((count, vocab), lambda k: (0, 0))],
        out_specs=pl.BlockSpec((step, vocab), lambda k: (k, 0)),
        out_shape=jax.ShapeDtypeStruct((depth, vocab), jnp.bfloat16),
        compiler_params=pltpu.CompilerParams(vmem_limit_bytes=40 * 2**20),
        cost_estimate=pl.CostEstimate(
            flops=2 * count * depth * vocab, bytes_accessed=2 * depth * (vocab + count), transcendentals=0
        ),
    )(*hidden, logit_grad)


def swap(value, distance, n):
    return lax.ppermute(value, "dp", [(i, i ^ distance) for i in range(n)])


def after(value, *done):
    return lax.optimization_barrier((value, *done))[0]


def gather_rows(teacher_rows, student_rows, n, prepared):
    far = jnp.concatenate([after(swap(teacher_rows, 8, n), *prepared), swap(student_rows, 8, n)], axis=1)
    rows = jnp.concatenate([teacher_rows, student_rows], axis=1)
    side = swap(rows, 2, n)
    near = swap(rows, 4, n)
    far_near = swap(far, 4, n)
    near_side = swap(near, 2, n)
    far_side = swap(far, 2, n)
    far_near_side = swap(far_near, 2, n)
    first = jnp.concatenate([rows, near, side, near_side], axis=0)
    second = jnp.concatenate([far, far_near, far_side, far_near_side], axis=0)
    return [first, second, swap(first, 1, n), swap(second, 1, n)]


def scatter_rows(keep, send, rows_local, n, grad_head):
    low = jnp.bfloat16
    full = jnp.float32
    held = keep + swap(send, 1, n).astype(full)
    quarter = 2 * rows_local
    near_keep, near_send, far_keep, far_send = (held[k * quarter : (k + 1) * quarter] for k in range(4))
    far_part = after(swap(far_send.astype(low), 2, n), grad_head)
    far = (far_keep + far_part.astype(full)).astype(low)
    near = near_keep + swap(near_send.astype(low), 2, n).astype(full)
    from_far = swap(far[:rows_local], 8, n)
    from_far_near = swap(far[rows_local:], 12, n)
    from_near = swap(near[rows_local:].astype(low), 4, n)
    return near[:rows_local] + from_far.astype(full) + from_far_near.astype(full) + from_near.astype(full)


def per_device(n, teacher_hidden, student_hidden, teacher_head, student_head, labels, order):
    rows_local, depth = student_hidden.shape
    tuned = xor_order(n) is not None and rows_local == 8
    me = lax.axis_index("dp").astype(jnp.int32).reshape(1)
    *heads, pick, label = prepare(me, order, labels, (teacher_head, student_head), rows_local, tuned)
    if tuned:
        hidden = gather_rows(teacher_hidden, student_hidden, n, (*heads, pick, label))
    else:
        rows = jnp.concatenate([teacher_hidden, student_hidden], axis=1)
        hidden = [lax.all_gather(rows, "dp", axis=0, tiled=True)]
    teacher_logits, student_logits, stats = logits(me, pick, label, hidden, heads, n, rows_local, tuned)
    stats = lax.all_to_all(stats, "dp", 0, 0)
    outs = gradient(me, label, stats, teacher_logits, student_logits, heads[1], rows_local, tuned)
    logit_grad, loss = outs[-2:]
    grad_head = head_gradient(hidden, logit_grad, depth)
    if tuned:
        grad_hidden = scatter_rows(outs[0], outs[1], rows_local, n, grad_head)
    else:
        grad_hidden = lax.psum_scatter(outs[0], "dp", scatter_dimension=0, tiled=True)
    return (loss[0, :rows_local], grad_hidden, grad_head)


def solution(mesh):
    in_specs = (
        P(("groups", "dp"), None),
        P(("groups", "dp"), None),
        P(None, "dp"),
        P(None, "dp"),
        P("groups"),
        P("groups"),
    )
    out_specs = (P(("groups", "dp")), P(("groups", "dp"), None), P("groups", "dp"))
    return jax.shard_map(
        functools.partial(per_device, mesh.shape["dp"]),
        mesh=mesh,
        in_specs=in_specs,
        out_specs=out_specs,
        check_vma=False,
    )
```

```python
import functools

import jax
import jax.numpy as jnp
from jax import lax
from jax.experimental import pallas as pl
from jax.experimental.pallas import tpu as pltpu
from jax.sharding import PartitionSpec as P

CE_WEIGHT = 0.5
FETCH_PARTS = 4
STATS = 8


def xor_order(n):
    return (0, 4, 2, 6, 8, 12, 10, 14, 1, 5, 3, 7, 9, 13, 11, 15) if n == 16 else None


def held_rows(shape, dim, me, rows_local, tuned):
    held = lax.broadcasted_iota(jnp.int32, shape, dim)
    if not tuned:
        return held
    step = rows_local.bit_length() - 1
    block = lax.shift_right_logical(held, step)
    bit = lambda k: lax.shift_right_logical(block, k) & 1
    distance = bit(3) + bit(2) * 8 + bit(1) * 2 + bit(0) * 4
    return (me ^ distance) * rows_local + (held & (rows_local - 1))


def to_column(is_row, row):
    return jnp.sum(jnp.where(is_row, row, 0.0), axis=1, keepdims=True)


def fetch_copies(source, target, sems):
    rows = source.shape[0] // sems.shape[0]
    parts = [pl.ds(k * rows, rows) for k in range(sems.shape[0])]
    return [pltpu.make_async_copy(source.at[part], target.at[part], sems.at[k]) for k, part in enumerate(parts)]


def fetch_kernel(after_ref, source, target, sems):
    copies = fetch_copies(source, target, sems)
    for copy in copies:
        copy.start()
    for copy in copies:
        copy.wait()


def prepare_kernel(
    rows_local, tuned, me_ref, order_ref, labels_ref, head_ref, head_out, pick_out, label_out, ids, id_sems, sems
):
    id_copies = [
        pltpu.make_async_copy(source, ids.at[j], id_sems.at[j]) for j, source in enumerate((order_ref, labels_ref))
    ]
    copies = fetch_copies(head_ref, head_out, sems)
    for copy in id_copies + copies:
        copy.start()
    me = me_ref[0]
    count = order_ref.shape[1]
    vocab = head_ref.shape[1]
    lanes = lax.broadcasted_iota(jnp.int32, (count, count), 1)
    is_row = held_rows((count, count), 0, me, rows_local, tuned) == lanes
    have = held_rows((count, count), 1, me, rows_local, tuned).astype(jnp.float32)
    for copy in id_copies:
        copy.wait()
    wanted = to_column(is_row, ids[0].astype(jnp.float32))
    pick_out[...] = jnp.where(wanted == have, 1.0, 0.0).astype(jnp.bfloat16)
    label = to_column(is_row, ids[1].astype(jnp.float32)) - (me * vocab).astype(jnp.float32)
    label_out[...] = jnp.broadcast_to(label, label_out.shape)
    for copy in copies:
        copy.wait()


def stay(value):
    return pltpu.with_memory_space_constraint(value, pltpu.HBM)


def fetch(me, head):
    return pl.pallas_call(
        fetch_kernel,
        in_specs=[pl.BlockSpec(memory_space=pltpu.SMEM), pl.BlockSpec(memory_space=pltpu.HBM)],
        out_specs=pl.BlockSpec(memory_space=pltpu.VMEM),
        out_shape=jax.ShapeDtypeStruct(head.shape, head.dtype),
        scratch_shapes=[pltpu.SemaphoreType.DMA((FETCH_PARTS,))],
        compiler_params=pltpu.CompilerParams(vmem_limit_bytes=24 * 2**20),
        cost_estimate=pl.CostEstimate(flops=0, bytes_accessed=head.size * 4, transcendentals=0),
    )(me, stay(head))


def prepare(me, order, labels, head, rows_local, tuned):
    count = order.shape[0]
    vmem = pl.BlockSpec(memory_space=pltpu.VMEM)
    hbm = pl.BlockSpec(memory_space=pltpu.HBM)
    return pl.pallas_call(
        functools.partial(prepare_kernel, rows_local, tuned),
        in_specs=[pl.BlockSpec(memory_space=pltpu.SMEM)] + [hbm] * 3,
        out_specs=(vmem,) * 3,
        out_shape=(
            jax.ShapeDtypeStruct(head.shape, head.dtype),
            jax.ShapeDtypeStruct((count, count), jnp.bfloat16),
            jax.ShapeDtypeStruct((count, 128), jnp.float32),
        ),
        scratch_shapes=[
            pltpu.VMEM((2, 1, count), jnp.int32),
            pltpu.SemaphoreType.DMA((2,)),
            pltpu.SemaphoreType.DMA((FETCH_PARTS,)),
        ],
        compiler_params=pltpu.CompilerParams(vmem_limit_bytes=24 * 2**20),
        cost_estimate=pl.CostEstimate(flops=0, bytes_accessed=head.size * 4, transcendentals=0),
    )(me, stay(order[None]), stay(labels[None]), stay(head))


def logits_kernel(rows_local, tuned, parts, me_ref, pick_ref, label_ref, *refs):
    pieces = refs[:parts]
    teacher_head, student_head, teacher_out, student_out, stats_out = refs[parts:]
    depth, vocab = student_head.shape

    def product(first, head):
        rows = jnp.concatenate([piece[:, first : first + depth] for piece in pieces], axis=0)
        return jnp.dot(rows, head[...], preferred_element_type=jnp.float32)

    me = me_ref[0]
    raw = product(0, teacher_head)
    student = product(depth, student_head)
    count = student.shape[0]
    high = raw.astype(jnp.bfloat16)
    rest = raw - high.astype(jnp.float32)
    middle = rest.astype(jnp.bfloat16)
    low = (rest - middle.astype(jnp.float32)).astype(jnp.bfloat16)
    pick = pick_ref[...]
    teacher = sum(jnp.dot(pick, piece, preferred_element_type=jnp.float32) for piece in (high, middle, low))
    teacher_out[...] = teacher
    student_out[...] = student
    is_label = label_ref[:, 0:1].astype(jnp.int32) == lax.broadcasted_iota(jnp.int32, (count, vocab), 1)
    teacher_max = jnp.max(teacher, axis=1, keepdims=True)
    student_max = jnp.max(student, axis=1, keepdims=True)
    teacher_exp = jnp.exp(teacher - teacher_max)
    values = (
        teacher_max,
        student_max,
        jnp.sum(teacher_exp, axis=1, keepdims=True),
        jnp.sum(jnp.exp(student - student_max), axis=1, keepdims=True),
        jnp.sum(teacher_exp * (teacher - student), axis=1, keepdims=True),
        jnp.sum(jnp.where(is_label, student, 0.0), axis=1, keepdims=True),
    )
    lanes = lax.broadcasted_iota(jnp.int32, (count, count), 1)
    is_row = held_rows((count, count), 0, me, rows_local, tuned) == lanes
    block = [jnp.sum(jnp.where(is_row, value, 0.0), axis=0, keepdims=True) for value in values]
    block.append(jnp.zeros((STATS - len(block), count), jnp.float32))
    stats_out[...] = jnp.broadcast_to(jnp.concatenate(block, axis=0)[None], stats_out.shape)


def logits(me, pick, label, hidden, heads, n, rows_local, tuned):
    count = pick.shape[0]
    depth, vocab = heads[0].shape
    vmem = pl.BlockSpec(memory_space=pltpu.VMEM)
    return pl.pallas_call(
        functools.partial(logits_kernel, rows_local, tuned, len(hidden)),
        in_specs=[pl.BlockSpec(memory_space=pltpu.SMEM)] + [vmem] * (4 + len(hidden)),
        out_specs=(vmem,) * 3,
        out_shape=(
            jax.ShapeDtypeStruct((count, vocab), jnp.float32),
            jax.ShapeDtypeStruct((count, vocab), jnp.float32),
            jax.ShapeDtypeStruct((n, STATS, count), jnp.float32),
        ),
        compiler_params=pltpu.CompilerParams(vmem_limit_bytes=40 * 2**20),
        cost_estimate=pl.CostEstimate(
            flops=4 * count * depth * vocab, bytes_accessed=4 * depth * (vocab + count), transcendentals=2 * count * vocab
        ),
    )(me, pick, label, *hidden, *heads)


def grad_kernel(
    rows_local, tuned, me_ref, label_ref, stats_ref, teacher_ref, student_ref, head_ref, keep_out, send_out, grad_out, loss_out
):
    me = me_ref[0]
    count, vocab = student_ref.shape
    devices = stats_ref.shape[0]
    top = stats_ref[0, 0:2]
    for d in range(1, devices):
        top = jnp.maximum(top, stats_ref[d, 0:2])
    totals = jnp.zeros((2, count), jnp.float32)
    cross = jnp.zeros((1, count), jnp.float32)
    label_logit = jnp.zeros((1, count), jnp.float32)
    for d in range(devices):
        weight = jnp.exp(stats_ref[d, 0:2] - top)
        totals += weight * stats_ref[d, 2:4]
        cross += weight[0:1] * stats_ref[d, 4:5]
        label_logit += stats_ref[d, 5:6]
    norms = top + jnp.log(totals)
    teacher_norm, student_norm = norms[0:1], norms[1:2]
    loss = cross / totals[0:1] - teacher_norm + student_norm + CE_WEIGHT * (student_norm - label_logit)
    lanes = lax.broadcasted_iota(jnp.int32, (count, count), 1)
    is_row = held_rows((count, count), 0, me, rows_local, tuned) == lanes
    mine = lax.broadcasted_iota(jnp.int32, (count, count), 0) + me * rows_local == lanes
    by_lane = lax.broadcasted_iota(jnp.int32, (count, count), 0) == lanes
    loss_out[...] = jnp.sum(jnp.where(by_lane, to_column(mine, loss), 0.0), axis=0, keepdims=True)
    is_label = label_ref[:, 0:1].astype(jnp.int32) == lax.broadcasted_iota(jnp.int32, (count, vocab), 1)
    grad = (
        (1.0 + CE_WEIGHT) * jnp.exp(student_ref[...] - to_column(is_row, student_norm))
        - jnp.exp(teacher_ref[...] - to_column(is_row, teacher_norm))
        - jnp.where(is_label, CE_WEIGHT, 0.0)
    ).astype(jnp.bfloat16)
    grad_out[...] = grad
    kept = keep_out.shape[0]
    depth = head_ref.shape[0]
    step = min(512, depth)
    for k in range(0, depth, step):
        part = lax.dot_general(
            grad, head_ref[k : k + step], (((1,), (1,)), ((), ())), preferred_element_type=jnp.float32
        )
        keep_out[:, k : k + step] = part[:kept]
        if send_out is not None:
            send_out[:, k : k + step] = part[kept:].astype(jnp.bfloat16)


def gradient(me, label, stats, teacher_logits, student_logits, head, rows_local, tuned):
    count, vocab = student_logits.shape
    depth = head.shape[0]
    kept = count // 2 if tuned else count
    vmem = pl.BlockSpec(memory_space=pltpu.VMEM)
    shapes = [jax.ShapeDtypeStruct((kept, depth), jnp.float32)]
    if tuned:
        shapes.append(jax.ShapeDtypeStruct((count - kept, depth), jnp.bfloat16))
    shapes += [jax.ShapeDtypeStruct((count, vocab), jnp.bfloat16), jax.ShapeDtypeStruct((1, count), jnp.float32)]

    def kernel(*refs):
        if tuned:
            grad_kernel(rows_local, tuned, *refs)
        else:
            grad_kernel(rows_local, tuned, *refs[:7], None, *refs[7:])

    return pl.pallas_call(
        kernel,
        in_specs=[pl.BlockSpec(memory_space=pltpu.SMEM)] + [vmem] * 5,
        out_specs=(vmem,) * len(shapes),
        out_shape=tuple(shapes),
        compiler_params=pltpu.CompilerParams(vmem_limit_bytes=40 * 2**20),
        cost_estimate=pl.CostEstimate(
            flops=2 * count * depth * vocab, bytes_accessed=2 * depth * (vocab + 2 * count), transcendentals=2 * count * vocab
        ),
    )(me, label, stats, teacher_logits, student_logits, head)


def head_kernel(parts, *refs):
    rows = jnp.concatenate([piece[...] for piece in refs[:parts]], axis=0)
    grad_ref, out_ref = refs[parts], refs[-1]
    out_ref[...] = lax.dot_general(
        rows, grad_ref[...], (((0,), (0,)), ((), ())), preferred_element_type=jnp.float32
    ).astype(jnp.bfloat16)


def head_gradient(hidden, logit_grad, depth, part, parts, written):
    count, vocab = logit_grad.shape
    step = min(512, depth)
    steps = depth // step // parts
    first = depth // step + part * steps
    more = () if written is None else (written,)
    return pl.pallas_call(
        functools.partial(head_kernel, len(hidden)),
        grid=(steps,),
        in_specs=[pl.BlockSpec((piece.shape[0], step), lambda k: (0, k + first)) for piece in hidden]
        + [pl.BlockSpec((count, vocab), lambda k: (0, 0))]
        + [pl.BlockSpec(memory_space=pl.ANY)] * len(more),
        out_specs=pl.BlockSpec((step, vocab), lambda k: (k + part * steps, 0)),
        out_shape=jax.ShapeDtypeStruct((depth, vocab), jnp.bfloat16),
        input_output_aliases={len(hidden) + 1: 0} if more else {},
        compiler_params=pltpu.CompilerParams(vmem_limit_bytes=40 * 2**20),
        cost_estimate=pl.CostEstimate(
            flops=2 * count * depth * vocab // parts,
            bytes_accessed=2 * depth * (vocab + count) // parts,
            transcendentals=0,
        ),
    )(*hidden, logit_grad, *more)


def swap(value, distance, n):
    return lax.ppermute(value, "dp", [(i, i ^ distance) for i in range(n)])


def after(value, *done):
    return lax.optimization_barrier((value, *done))[0]


def gather_rows(teacher_rows, student_rows, n, teacher_fetch, student_fetch):
    join = lambda pair: jnp.concatenate(pair, axis=1)
    both = (teacher_rows, student_rows)
    far = [swap(rows, 8, n) for rows in both]
    near = [swap(rows, 4, n) for rows in both]
    side = [swap(rows, 2, n) for rows in both]
    teacher_fetched = teacher_fetch(None)
    far[0] = after(far[0], *side, *teacher_fetched)
    far_near = [swap(rows, 4, n) for rows in far]
    far_side = [swap(rows, 2, n) for rows in far]
    near_side = swap(join(near), 2, n)
    far_near_side = [swap(rows, 2, n) for rows in far_near]
    first = jnp.concatenate([join(both), join(near), join(side), near_side], axis=0)
    second = jnp.concatenate([join(far), join(far_near), join(far_side), join(far_near_side)], axis=0)
    student_fetched = student_fetch(far_near_side[1])
    return [first, second, swap(first, 1, n), swap(second, 1, n)], teacher_fetched, student_fetched


def scatter_rows(keep, send, logit_grad, rows_local, n, head_parts):
    low = jnp.bfloat16
    full = jnp.float32
    half = 2 * rows_local
    other = swap(send, 1, n)
    held = keep + other.astype(full)
    near_keep, near_send, far_keep, far_send = (held[k * half : (k + 1) * half] for k in range(4))
    near_keep, near_send, far_keep, far_send = lax.optimization_barrier(
        (near_keep, near_send.astype(low), far_keep, far_send.astype(low))
    )
    far_other = swap(far_send, 2, n)
    part = head_parts(0, after(logit_grad, other), None)
    near_other = swap(after(near_send, part), 2, n)
    far = (far_keep + far_other.astype(full)).astype(low)
    from_far = swap(far[:rows_local], 8, n)
    from_far_near = swap(far[rows_local:], 12, n)
    grad_head = head_parts(1, after(logit_grad, far_other), part)
    near = near_keep + after(near_other, grad_head).astype(full)
    from_near = swap(near[rows_local:].astype(low), 4, n)
    total = near[:rows_local] + from_far.astype(full) + from_far_near.astype(full) + from_near.astype(full)
    return total, grad_head


def per_device(n, teacher_hidden, student_hidden, teacher_head, student_head, labels, order):
    rows_local, depth = student_hidden.shape
    tuned = xor_order(n) is not None and rows_local == 8
    me = lax.axis_index("dp").astype(jnp.int32).reshape(1)
    teacher_fetch = lambda done: prepare(me if done is None else after(me, done), order, labels, teacher_head, rows_local, tuned)
    student_fetch = lambda done: fetch(after(me, done), student_head)
    if tuned:
        hidden, *fetched = gather_rows(teacher_hidden, student_hidden, n, teacher_fetch, student_fetch)
    else:
        fetched = teacher_fetch(me), student_fetch(me)
        rows = jnp.concatenate([teacher_hidden, student_hidden], axis=1)
        hidden = [lax.all_gather(rows, "dp", axis=0, tiled=True)]
    (teacher_head, pick, label), student_head = fetched
    heads = (teacher_head, student_head)
    teacher_logits, student_logits, stats = logits(me, pick, label, hidden, heads, n, rows_local, tuned)
    stats = lax.all_to_all(stats, "dp", 0, 0)
    outs = gradient(me, label, stats, teacher_logits, student_logits, heads[1], rows_local, tuned)
    logit_grad, loss = outs[-2:]
    if tuned:
        head_parts = lambda part, logit_grad, written: head_gradient(hidden, logit_grad, depth, part, 2, written)
        grad_hidden, grad_head = scatter_rows(outs[0], outs[1], logit_grad, rows_local, n, head_parts)
    else:
        grad_head = head_gradient(hidden, logit_grad, depth, 0, 1, None)
        grad_hidden = lax.psum_scatter(outs[0], "dp", scatter_dimension=0, tiled=True)
    return (loss[0, :rows_local], grad_hidden, grad_head)


def solution(mesh):
    in_specs = (
        P(("groups", "dp"), None),
        P(("groups", "dp"), None),
        P(None, "dp"),
        P(None, "dp"),
        P("groups"),
        P("groups"),
    )
    out_specs = (P(("groups", "dp")), P(("groups", "dp"), None), P("groups", "dp"))
    return jax.shard_map(
        functools.partial(per_device, mesh.shape["dp"]),
        mesh=mesh,
        in_specs=in_specs,
        out_specs=out_specs,
        check_vma=False,
    )
```

```python
import functools

import jax
import jax.numpy as jnp
from jax import lax
from jax.experimental import pallas as pl
from jax.experimental.pallas import tpu as pltpu
from jax.sharding import PartitionSpec as P

CE_WEIGHT = 0.5
STATS = 8


def held_rows(shape, dim, me, rows_local, tuned):
    held = lax.broadcasted_iota(jnp.int32, shape, dim)
    if not tuned:
        return held
    step = rows_local.bit_length() - 1
    block = lax.shift_right_logical(held, step)
    distance = (block & 7) * 2 + lax.shift_right_logical(block, 3)
    return (me ^ distance) * rows_local + (held & (rows_local - 1))


def to_column(is_row, row):
    return jnp.sum(jnp.where(is_row, row, 0.0), axis=1, keepdims=True)


def prepare_kernel(
    rows_local, tuned, me_ref, order_ref, labels_ref, *refs
):
    sources, targets = refs[:2], refs[2:4]
    pick_out, label_out, ids, id_sems, sems = refs[4:]
    id_copies = [
        pltpu.make_async_copy(source, ids.at[j], id_sems.at[j]) for j, source in enumerate((order_ref, labels_ref))
    ]
    copies = [pltpu.make_async_copy(source, target, sems.at[j]) for j, (source, target) in enumerate(zip(sources, targets))]
    for copy in id_copies + copies:
        copy.start()
    me = me_ref[0]
    count = order_ref.shape[1]
    vocab = sources[0].shape[1]
    lanes = lax.broadcasted_iota(jnp.int32, (count, count), 1)
    is_row = held_rows((count, count), 0, me, rows_local, tuned) == lanes
    have = held_rows((count, count), 1, me, rows_local, tuned).astype(jnp.float32)
    for copy in id_copies:
        copy.wait()
    wanted = to_column(is_row, ids[0].astype(jnp.float32))
    pick_out[...] = jnp.where(wanted == have, 1.0, 0.0).astype(jnp.bfloat16)
    label = to_column(is_row, ids[1].astype(jnp.float32)) - (me * vocab).astype(jnp.float32)
    label_out[...] = jnp.broadcast_to(label, label_out.shape)
    for copy in copies:
        copy.wait()


def stay(value):
    return pltpu.with_memory_space_constraint(value, pltpu.HBM)


def prepare(me, order, labels, heads, rows_local, tuned):
    count = order.shape[0]
    vmem = pl.BlockSpec(memory_space=pltpu.VMEM)
    hbm = pl.BlockSpec(memory_space=pltpu.HBM)
    return pl.pallas_call(
        functools.partial(prepare_kernel, rows_local, tuned),
        in_specs=[pl.BlockSpec(memory_space=pltpu.SMEM)] + [hbm] * 4,
        out_specs=(vmem,) * 4,
        out_shape=(
            jax.ShapeDtypeStruct(heads[0].shape, heads[0].dtype),
            jax.ShapeDtypeStruct(heads[1].shape, heads[1].dtype),
            jax.ShapeDtypeStruct((count, count), jnp.bfloat16),
            jax.ShapeDtypeStruct((count, 128), jnp.float32),
        ),
        scratch_shapes=[
            pltpu.VMEM((2, 1, count), jnp.int32),
            pltpu.SemaphoreType.DMA((2,)),
            pltpu.SemaphoreType.DMA((2,)),
        ],
        compiler_params=pltpu.CompilerParams(vmem_limit_bytes=24 * 2**20),
        cost_estimate=pl.CostEstimate(flops=0, bytes_accessed=heads[0].size * 8, transcendentals=0),
    )(me, stay(order[None]), stay(labels[None]), *map(stay, heads))


def logits_kernel(rows_local, tuned, parts, me_ref, pick_ref, label_ref, *refs):
    pieces = refs[:parts]
    teacher_head, student_head, teacher_out, student_out, stats_out = refs[parts:]
    depth, vocab = student_head.shape

    def product(first, head):
        rows = jnp.concatenate([piece[:, first : first + depth] for piece in pieces], axis=0)
        return jnp.dot(rows, head[...], preferred_element_type=jnp.float32)

    me = me_ref[0]
    raw = product(0, teacher_head)
    student = product(depth, student_head)
    count = student.shape[0]
    high = raw.astype(jnp.bfloat16)
    rest = raw - high.astype(jnp.float32)
    middle = rest.astype(jnp.bfloat16)
    low = (rest - middle.astype(jnp.float32)).astype(jnp.bfloat16)
    pick = pick_ref[...]
    teacher = sum(jnp.dot(pick, piece, preferred_element_type=jnp.float32) for piece in (high, middle, low))
    teacher_out[...] = teacher
    student_out[...] = student
    is_label = label_ref[:, 0:1].astype(jnp.int32) == lax.broadcasted_iota(jnp.int32, (count, vocab), 1)
    teacher_max = jnp.max(teacher, axis=1, keepdims=True)
    student_max = jnp.max(student, axis=1, keepdims=True)
    teacher_exp = jnp.exp(teacher - teacher_max)
    values = (
        teacher_max,
        student_max,
        jnp.sum(teacher_exp, axis=1, keepdims=True),
        jnp.sum(jnp.exp(student - student_max), axis=1, keepdims=True),
        jnp.sum(teacher_exp * (teacher - student), axis=1, keepdims=True),
        jnp.sum(jnp.where(is_label, student, 0.0), axis=1, keepdims=True),
    )
    lanes = lax.broadcasted_iota(jnp.int32, (count, count), 1)
    is_row = held_rows((count, count), 0, me, rows_local, tuned) == lanes
    block = [jnp.sum(jnp.where(is_row, value, 0.0), axis=0, keepdims=True) for value in values]
    block.append(jnp.zeros((STATS - len(block), count), jnp.float32))
    stats_out[...] = jnp.broadcast_to(jnp.concatenate(block, axis=0)[None], stats_out.shape)


def logits(me, pick, label, hidden, heads, n, rows_local, tuned):
    count = pick.shape[0]
    depth, vocab = heads[0].shape
    vmem = pl.BlockSpec(memory_space=pltpu.VMEM)
    return pl.pallas_call(
        functools.partial(logits_kernel, rows_local, tuned, len(hidden)),
        in_specs=[pl.BlockSpec(memory_space=pltpu.SMEM)] + [vmem] * (4 + len(hidden)),
        out_specs=(vmem,) * 3,
        out_shape=(
            jax.ShapeDtypeStruct((count, vocab), jnp.float32),
            jax.ShapeDtypeStruct((count, vocab), jnp.float32),
            jax.ShapeDtypeStruct((n, STATS, count), jnp.float32),
        ),
        compiler_params=pltpu.CompilerParams(vmem_limit_bytes=40 * 2**20),
        cost_estimate=pl.CostEstimate(
            flops=4 * count * depth * vocab, bytes_accessed=4 * depth * (vocab + count), transcendentals=2 * count * vocab
        ),
    )(me, pick, label, *hidden, *heads)


def grad_kernel(
    rows_local, tuned, me_ref, label_ref, stats_ref, teacher_ref, student_ref, head_ref, keep_out, near_out, far_out, grad_out, loss_out
):
    me = me_ref[0]
    count, vocab = student_ref.shape
    devices = stats_ref.shape[0]
    top = stats_ref[0, 0:2]
    for d in range(1, devices):
        top = jnp.maximum(top, stats_ref[d, 0:2])
    totals = jnp.zeros((2, count), jnp.float32)
    cross = jnp.zeros((1, count), jnp.float32)
    label_logit = jnp.zeros((1, count), jnp.float32)
    for d in range(devices):
        weight = jnp.exp(stats_ref[d, 0:2] - top)
        totals += weight * stats_ref[d, 2:4]
        cross += weight[0:1] * stats_ref[d, 4:5]
        label_logit += stats_ref[d, 5:6]
    norms = top + jnp.log(totals)
    teacher_norm, student_norm = norms[0:1], norms[1:2]
    loss = cross / totals[0:1] - teacher_norm + student_norm + CE_WEIGHT * (student_norm - label_logit)
    lanes = lax.broadcasted_iota(jnp.int32, (count, count), 1)
    is_row = held_rows((count, count), 0, me, rows_local, tuned) == lanes
    mine = lax.broadcasted_iota(jnp.int32, (count, count), 0) + me * rows_local == lanes
    by_lane = lax.broadcasted_iota(jnp.int32, (count, count), 0) == lanes
    loss_out[...] = jnp.sum(jnp.where(by_lane, to_column(mine, loss), 0.0), axis=0, keepdims=True)
    is_label = label_ref[:, 0:1].astype(jnp.int32) == lax.broadcasted_iota(jnp.int32, (count, vocab), 1)
    grad = (
        (1.0 + CE_WEIGHT) * jnp.exp(student_ref[...] - to_column(is_row, student_norm))
        - jnp.exp(teacher_ref[...] - to_column(is_row, teacher_norm))
        - jnp.where(is_label, CE_WEIGHT, 0.0)
    ).astype(jnp.bfloat16)
    grad_out[...] = grad
    kept = keep_out.shape[0]
    depth = head_ref.shape[0]
    step = min(512, depth)
    for k in range(0, depth, step):
        part = lax.dot_general(
            grad, head_ref[k : k + step], (((1,), (1,)), ((), ())), preferred_element_type=jnp.float32
        )
        keep_out[:, k : k + step] = part[:kept]
        if kept < count:
            half = kept // 2
            near_out[:, k : k + step] = part[kept : kept + half].astype(jnp.bfloat16)
            far_out[:, k : k + step] = part[kept + half :].astype(jnp.bfloat16)


def gradient(me, label, stats, teacher_logits, student_logits, head, rows_local, tuned):
    count, vocab = student_logits.shape
    depth = head.shape[0]
    kept = count // 2 if tuned else count
    vmem = pl.BlockSpec(memory_space=pltpu.VMEM)
    shapes = [jax.ShapeDtypeStruct((kept, depth), jnp.float32)]
    if tuned:
        shapes += [jax.ShapeDtypeStruct(((count - kept) // 2, depth), jnp.bfloat16)] * 2
    shapes += [jax.ShapeDtypeStruct((count, vocab), jnp.bfloat16), jax.ShapeDtypeStruct((1, count), jnp.float32)]

    def kernel(*refs):
        if tuned:
            grad_kernel(rows_local, tuned, *refs)
        else:
            grad_kernel(rows_local, tuned, *refs[:7], None, None, *refs[7:])

    return pl.pallas_call(
        kernel,
        in_specs=[pl.BlockSpec(memory_space=pltpu.SMEM)] + [vmem] * 5,
        out_specs=(vmem,) * len(shapes),
        out_shape=tuple(shapes),
        compiler_params=pltpu.CompilerParams(vmem_limit_bytes=40 * 2**20),
        cost_estimate=pl.CostEstimate(
            flops=2 * count * depth * vocab, bytes_accessed=2 * depth * (vocab + 2 * count), transcendentals=2 * count * vocab
        ),
    )(me, label, stats, teacher_logits, student_logits, head)


def head_kernel(parts, *refs):
    grad_ref, out_ref, held, sems = refs[parts:]
    steps, step, _ = held.shape
    copies = []
    for k in range(steps):
        first = (steps + k) * step
        rows = jnp.concatenate([piece[:, first : first + step] for piece in refs[:parts]], axis=0)
        held[k] = lax.dot_general(
            rows, grad_ref[...], (((0,), (0,)), ((), ())), preferred_element_type=jnp.float32
        ).astype(jnp.bfloat16)
        copies.append(pltpu.make_async_copy(held.at[k], out_ref.at[pl.ds(k * step, step)], sems.at[k]))
        copies[-1].start()
    for copy in copies:
        copy.wait()


def head_gradient(hidden, logit_grad, depth):
    count, vocab = logit_grad.shape
    step = min(256, depth)
    return pl.pallas_call(
        functools.partial(head_kernel, len(hidden)),
        in_specs=[pl.BlockSpec(memory_space=pltpu.VMEM)] * (len(hidden) + 1),
        out_specs=pl.BlockSpec(memory_space=pltpu.HBM),
        out_shape=jax.ShapeDtypeStruct((depth, vocab), jnp.bfloat16),
        scratch_shapes=[
            pltpu.VMEM((depth // step, step, vocab), jnp.bfloat16),
            pltpu.SemaphoreType.DMA((depth // step,)),
        ],
        compiler_params=pltpu.CompilerParams(vmem_limit_bytes=24 * 2**20),
        cost_estimate=pl.CostEstimate(
            flops=2 * count * depth * vocab, bytes_accessed=2 * depth * (vocab + count), transcendentals=0
        ),
    )(*hidden, logit_grad)


def swap(value, distance, n):
    return lax.ppermute(value, "dp", [(i, i ^ distance) for i in range(n)])


def after(value, *done):
    return lax.optimization_barrier((value, *done))[0]


def join_kernel(teacher_ref, student_ref, out_ref, sems):
    depth = teacher_ref.shape[1]
    copies = [
        pltpu.make_async_copy(ref, out_ref.at[:, pl.ds(j * depth, depth)], sems.at[j])
        for j, ref in enumerate((teacher_ref, student_ref))
    ]
    for copy in copies:
        copy.start()
    for copy in copies:
        copy.wait()


def join_rows(teacher_rows, student_rows):
    count, depth = teacher_rows.shape
    return pl.pallas_call(
        join_kernel,
        in_specs=[pl.BlockSpec(memory_space=pltpu.HBM)] * 2,
        out_specs=pl.BlockSpec(memory_space=pltpu.VMEM),
        out_shape=jax.ShapeDtypeStruct((count, 2 * depth), teacher_rows.dtype),
        scratch_shapes=[pltpu.SemaphoreType.DMA((2,))],
        compiler_params=pltpu.CompilerParams(vmem_limit_bytes=2**20),
        cost_estimate=pl.CostEstimate(flops=0, bytes_accessed=8 * count * depth, transcendentals=0),
    )(stay(teacher_rows), stay(student_rows))


def gather_rows(teacher_rows, student_rows, n, fetch):
    join = lambda pair: jnp.concatenate(pair, axis=1)
    stack = lambda *parts: jnp.concatenate(parts, axis=0)
    far = join((swap(teacher_rows, 8, n), swap(student_rows, 8, n)))
    rows = join_rows(teacher_rows, student_rows)
    near, side = swap(rows, 4, n), swap(rows, 2, n)
    fetched = fetch(rows)
    far = after(far, *fetched)
    far_near = swap(far, 4, n)
    near_side = swap(near, 2, n)
    far_side = swap(far, 2, n)
    far_near_side = swap(far_near, 2, n)
    held = [stack(rows, side, near, near_side), stack(far, far_side, far_near, far_near_side)]
    return held + [swap(piece, 1, n) for piece in held], fetched


def scatter_rows(keep, sends, logit_grad, rows_local, n, head_gradient_of):
    low = jnp.bfloat16
    full = jnp.float32
    others = [swap(send, 1, n) for send in sends[::-1]][::-1]

    def split(half):
        count = keep.shape[0] // 2
        held = keep[half * count : (half + 1) * count] + others[half].astype(full)
        held = held.reshape(2, 2, rows_local, -1)
        take = lambda side: held[:, side].reshape(2 * rows_local, -1)
        return lax.optimization_barrier((take(0), take(1).astype(low)))

    far_keep, far_send = split(1)
    far_other = swap(far_send, 2, n)
    grad_head = head_gradient_of(after(logit_grad, others[1]))
    others[0] = after(others[0], far_send)
    near_keep, near_send = split(0)
    near_other = swap(after(near_send, grad_head), 2, n)
    far = (far_keep + far_other.astype(full)).astype(low)
    from_far = swap(far[:rows_local], 8, n)
    from_far_near = swap(far[rows_local:], 12, n)
    near = near_keep + near_other.astype(full)
    from_near = swap(near[rows_local:].astype(low), 4, n)
    total = near[:rows_local] + from_far.astype(full) + from_far_near.astype(full) + from_near.astype(full)
    return total, grad_head


def per_device(n, teacher_hidden, student_hidden, teacher_head, student_head, labels, order):
    rows_local, depth = student_hidden.shape
    tuned = n == 16 and rows_local == 8
    me = lax.axis_index("dp").astype(jnp.int32).reshape(1)
    heads = (teacher_head, student_head)
    fetch = lambda *done: prepare(after(me, *done), order, labels, heads, rows_local, tuned)
    if tuned:
        hidden, fetched = gather_rows(teacher_hidden, student_hidden, n, fetch)
    else:
        fetched = fetch(me)
        rows = jnp.concatenate([teacher_hidden, student_hidden], axis=1)
        hidden = [lax.all_gather(rows, "dp", axis=0, tiled=True)]
    *heads, pick, label = fetched
    teacher_logits, student_logits, stats = logits(me, pick, label, hidden, heads, n, rows_local, tuned)
    stats = lax.all_to_all(stats, "dp", 0, 0)
    outs = gradient(me, label, stats, teacher_logits, student_logits, heads[1], rows_local, tuned)
    logit_grad, loss = outs[-2:]
    head_gradient_of = lambda logit_grad: head_gradient(hidden, logit_grad, depth)
    if tuned:
        grad_hidden, grad_head = scatter_rows(outs[0], outs[1:3], logit_grad, rows_local, n, head_gradient_of)
    else:
        grad_head = head_gradient_of(logit_grad)
        grad_hidden = lax.psum_scatter(outs[0], "dp", scatter_dimension=0, tiled=True)
    return (loss[0, :rows_local], grad_hidden, grad_head)


def solution(mesh):
    in_specs = (
        P(("groups", "dp"), None),
        P(("groups", "dp"), None),
        P(None, "dp"),
        P(None, "dp"),
        P("groups"),
        P("groups"),
    )
    out_specs = (P(("groups", "dp")), P(("groups", "dp"), None), P("groups", "dp"))
    return jax.shard_map(
        functools.partial(per_device, mesh.shape["dp"]),
        mesh=mesh,
        in_specs=in_specs,
        out_specs=out_specs,
        check_vma=False,
    )
```

```python
import functools

import jax
import jax.numpy as jnp
from jax import lax
from jax.experimental import pallas as pl
from jax.experimental.pallas import tpu as pltpu
from jax.sharding import PartitionSpec as P

CE_WEIGHT = 0.5
VMEM_LIMIT = 28 * 2**20
STATS = 8


def held_rows(shape, dim, me, rows_local, tuned):
    held = lax.broadcasted_iota(jnp.int32, shape, dim)
    if not tuned:
        return held
    step = rows_local.bit_length() - 1
    block = lax.shift_right_logical(held, step)
    distance = (block & 7) * 2 + lax.shift_right_logical(block, 3)
    return (me ^ distance) * rows_local + (held & (rows_local - 1))


def to_column(is_row, row):
    return jnp.sum(jnp.where(is_row, row, 0.0), axis=1, keepdims=True)


def prepare_kernel(rows_local, tuned, me_ref, order_ref, labels_ref, *refs):
    teacher_ref, student_ref, teacher_out, student_out, pick_out, label_out, *turned_out = refs[: -4]
    ids, id_sems, teacher_sem, student_sems = refs[-4:]
    id_copies = [
        pltpu.make_async_copy(source, ids.at[j], id_sems.at[j]) for j, source in enumerate((order_ref, labels_ref))
    ]
    pieces = student_sems.shape[0]
    rows = student_ref.shape[0] // pieces
    parts = [pl.ds(k * rows, rows) for k in range(pieces)]
    copies = [
        pltpu.make_async_copy(student_ref.at[part], student_out.at[part], student_sems.at[k])
        for k, part in enumerate(parts)
    ]
    copies.append(pltpu.make_async_copy(teacher_ref, teacher_out, teacher_sem))
    for copy in id_copies + copies:
        copy.start()
    me = me_ref[0]
    count = order_ref.shape[1]
    vocab = teacher_ref.shape[1]
    lanes = lax.broadcasted_iota(jnp.int32, (count, count), 1)
    is_row = held_rows((count, count), 0, me, rows_local, tuned) == lanes
    have = held_rows((count, count), 1, me, rows_local, tuned).astype(jnp.float32)
    for copy in id_copies:
        copy.wait()
    wanted = to_column(is_row, ids[0].astype(jnp.float32))
    pick_out[...] = jnp.where(wanted == have, 1.0, 0.0).astype(jnp.bfloat16)
    label = to_column(is_row, ids[1].astype(jnp.float32)) - (me * vocab).astype(jnp.float32)
    label_out[...] = jnp.broadcast_to(label, label_out.shape)
    for k, copy in enumerate(copies):
        copy.wait()
        if k < pieces:
            for out in turned_out:
                out[:, k * rows : (k + 1) * rows] = student_out[k * rows : (k + 1) * rows].T


def stay(value):
    return pltpu.with_memory_space_constraint(value, pltpu.HBM)


def prepare(me, order, labels, heads, rows_local, tuned):
    count = order.shape[0]
    vmem = pl.BlockSpec(memory_space=pltpu.VMEM)
    hbm = pl.BlockSpec(memory_space=pltpu.HBM)
    shapes = [
        jax.ShapeDtypeStruct(heads[0].shape, heads[0].dtype),
        jax.ShapeDtypeStruct(heads[1].shape, heads[1].dtype),
        jax.ShapeDtypeStruct((count, count), jnp.bfloat16),
        jax.ShapeDtypeStruct((count, 128), jnp.float32),
    ] + [jax.ShapeDtypeStruct(heads[1].shape[::-1], heads[1].dtype)] * tuned
    return pl.pallas_call(
        functools.partial(prepare_kernel, rows_local, tuned),
        in_specs=[pl.BlockSpec(memory_space=pltpu.SMEM)] + [hbm] * 4,
        out_specs=(vmem,) * len(shapes),
        out_shape=tuple(shapes),
        scratch_shapes=[
            pltpu.VMEM((2, 1, count), jnp.int32),
            pltpu.SemaphoreType.DMA((2,)),
            pltpu.SemaphoreType.DMA,
            pltpu.SemaphoreType.DMA((8,)),
        ],
        compiler_params=pltpu.CompilerParams(vmem_limit_bytes=24 * 2**20),
        cost_estimate=pl.CostEstimate(flops=0, bytes_accessed=heads[0].size * 8, transcendentals=0),
    )(me, stay(order[None]), stay(labels[None]), *map(stay, heads))


def logits_kernel(rows_local, tuned, parts, me_ref, pick_ref, label_ref, *refs):
    pieces = refs[:parts]
    teacher_head, student_head, teacher_out, student_out, stats_out, *away_out = refs[parts:]
    depth, vocab = student_head.shape

    def product(first, head):
        rows = jnp.concatenate([piece[:, first : first + depth] for piece in pieces], axis=0)
        return jnp.dot(rows, head[...], preferred_element_type=jnp.float32)

    me = me_ref[0]
    raw = product(0, teacher_head)
    student = product(depth, student_head)
    count = student.shape[0]
    high = raw.astype(jnp.bfloat16)
    rest = raw - high.astype(jnp.float32)
    middle = rest.astype(jnp.bfloat16)
    low = (rest - middle.astype(jnp.float32)).astype(jnp.bfloat16)
    pick = pick_ref[...]
    teacher = sum(jnp.dot(pick, piece, preferred_element_type=jnp.float32) for piece in (high, middle, low))
    teacher_out[...] = teacher
    student_out[...] = student
    for out in away_out:
        out[0] = teacher[count // 2 :]
        out[1] = student[count // 2 :]
    is_label = label_ref[:, 0:1].astype(jnp.int32) == lax.broadcasted_iota(jnp.int32, (count, vocab), 1)
    teacher_max = jnp.max(teacher, axis=1, keepdims=True)
    student_max = jnp.max(student, axis=1, keepdims=True)
    teacher_exp = jnp.exp(teacher - teacher_max)
    values = (
        teacher_max,
        student_max,
        jnp.sum(teacher_exp, axis=1, keepdims=True),
        jnp.sum(jnp.exp(student - student_max), axis=1, keepdims=True),
        jnp.sum(teacher_exp * (teacher - student), axis=1, keepdims=True),
        jnp.sum(jnp.where(is_label, student, 0.0), axis=1, keepdims=True),
    )
    lanes = lax.broadcasted_iota(jnp.int32, (count, count), 1)
    is_row = held_rows((count, count), 0, me, rows_local, tuned) == lanes
    block = [jnp.sum(jnp.where(is_row, value, 0.0), axis=0, keepdims=True) for value in values]
    block.append(jnp.zeros((STATS - len(block), count), jnp.float32))
    stats_out[...] = jnp.broadcast_to(jnp.concatenate(block, axis=0)[None], stats_out.shape)


def logits(me, pick, label, hidden, heads, n, rows_local, tuned):
    count = pick.shape[0]
    depth, vocab = heads[0].shape
    vmem = pl.BlockSpec(memory_space=pltpu.VMEM)
    shapes = [(count, vocab), (count, vocab), (n, STATS, count)] + [(2, count // 2, vocab)] * tuned
    return pl.pallas_call(
        functools.partial(logits_kernel, rows_local, tuned, len(hidden)),
        in_specs=[pl.BlockSpec(memory_space=pltpu.SMEM)] + [vmem] * (4 + len(hidden)),
        out_specs=(vmem,) * len(shapes),
        out_shape=tuple(jax.ShapeDtypeStruct(shape, jnp.float32) for shape in shapes),
        compiler_params=pltpu.CompilerParams(vmem_limit_bytes=VMEM_LIMIT),
        cost_estimate=pl.CostEstimate(
            flops=4 * count * depth * vocab, bytes_accessed=4 * depth * (vocab + count), transcendentals=2 * count * vocab
        ),
    )(me, pick, label, *hidden, *heads)


def merged(stats_ref):
    devices, _, count = stats_ref.shape
    top = stats_ref[0, 0:2]
    for d in range(1, devices):
        top = jnp.maximum(top, stats_ref[d, 0:2])
    totals = jnp.zeros((2, count), jnp.float32)
    cross = jnp.zeros((1, count), jnp.float32)
    label_logit = jnp.zeros((1, count), jnp.float32)
    for d in range(devices):
        weight = jnp.exp(stats_ref[d, 0:2] - top)
        totals += weight * stats_ref[d, 2:4]
        cross += weight[0:1] * stats_ref[d, 4:5]
        label_logit += stats_ref[d, 5:6]
    return top + jnp.log(totals), totals, cross, label_logit


def logit_gradient(teacher, student, norms, is_row, label):
    is_label = label.astype(jnp.int32) == lax.broadcasted_iota(jnp.int32, student.shape, 1)
    return (
        (1.0 + CE_WEIGHT) * jnp.exp(student - to_column(is_row, norms[1:2]))
        - jnp.exp(teacher - to_column(is_row, norms[0:1]))
        - jnp.where(is_label, CE_WEIGHT, 0.0)
    ).astype(jnp.bfloat16)


def times_transposed(grad, head):
    return lax.dot_general(grad, head, (((1,), (1,)), ((), ())), preferred_element_type=jnp.float32)


def grad_kernel(
    rows_local, me_ref, label_ref, stats_ref, teacher_ref, student_ref, away_ref, turned_ref, other_ref, *outs
):
    near_keep, near_send, far_keep, far_send = outs
    me = me_ref[0]
    count, vocab = student_ref.shape
    own = count // 2
    norms = merged(stats_ref)[0]
    is_row = held_rows((own, count), 0, me, rows_local, True) == lax.broadcasted_iota(jnp.int32, (own, count), 1)
    label = label_ref[:own, 0:1]
    grad = logit_gradient(teacher_ref[:own], student_ref[:own], norms, is_row, label)
    shift = jnp.where((me & 1) == 0, -vocab, vocab).astype(jnp.float32)
    other = logit_gradient(away_ref[0], away_ref[1], norms, is_row, label + shift)
    depth = turned_ref.shape[1]
    step = min(512, depth)
    for k in range(0, depth, step):
        part = jnp.dot(grad, turned_ref[:, k : k + step], preferred_element_type=jnp.float32)
        part += jnp.dot(other, other_ref[:, k : k + step], preferred_element_type=jnp.float32)
        blocks = [part[b * rows_local : (b + 1) * rows_local] for b in range(8)]
        for j, out in enumerate((near_keep, near_send, far_keep, far_send)):
            first = (j // 2) * 4 + j % 2
            out[:, k : k + step] = jnp.concatenate((blocks[first], blocks[first + 2]), axis=0).astype(out.dtype)


def whole_grad_kernel(rows_local, me_ref, label_ref, stats_ref, teacher_ref, student_ref, head_ref, out_ref):
    count, vocab = student_ref.shape
    norms = merged(stats_ref)[0]
    is_row = held_rows((count, count), 0, me_ref[0], rows_local, False) == lax.broadcasted_iota(
        jnp.int32, (count, count), 1
    )
    grad = logit_gradient(teacher_ref[...], student_ref[...], norms, is_row, label_ref[:, 0:1])
    depth = head_ref.shape[0]
    step = min(512, depth)
    for k in range(0, depth, step):
        out_ref[:, k : k + step] = times_transposed(grad, head_ref[k : k + step])


def gradient(me, label, stats, logits, heads, rows_local, tuned):
    count, vocab = logits[0].shape
    depth = heads[0].shape[1 if tuned else 0]
    vmem = pl.BlockSpec(memory_space=pltpu.VMEM)
    if tuned:
        shapes = [jax.ShapeDtypeStruct((2 * rows_local, depth), kind) for kind in (jnp.float32, jnp.bfloat16)] * 2
    else:
        shapes = [jax.ShapeDtypeStruct((count, depth), jnp.float32)]
    return pl.pallas_call(
        functools.partial(grad_kernel if tuned else whole_grad_kernel, rows_local),
        in_specs=[pl.BlockSpec(memory_space=pltpu.SMEM)] + [vmem] * (2 + len(logits) + len(heads)),
        out_specs=(vmem,) * len(shapes),
        out_shape=tuple(shapes),
        compiler_params=pltpu.CompilerParams(vmem_limit_bytes=VMEM_LIMIT),
        cost_estimate=pl.CostEstimate(
            flops=2 * count * depth * vocab, bytes_accessed=2 * depth * (vocab + 2 * count), transcendentals=2 * count * vocab
        ),
    )(me, label, stats, *logits, *heads)


def head_kernel(rows_local, tuned, me_ref, label_ref, stats_ref, teacher_ref, student_ref, *refs):
    *pieces, out_ref, loss_out, held, sems = refs
    me = me_ref[0]
    count = student_ref.shape[0]
    lanes = lax.broadcasted_iota(jnp.int32, (count, count), 1)
    is_row = held_rows((count, count), 0, me, rows_local, tuned) == lanes
    norms, totals, cross, label_logit = merged(stats_ref)
    grad = logit_gradient(teacher_ref[...], student_ref[...], norms, is_row, label_ref[:, 0:1])
    steps, step, _ = held.shape
    copies = []
    for k in range(steps):
        first = (steps + k) * step
        rows = jnp.concatenate([piece[:, first : first + step] for piece in pieces], axis=0)
        held[k] = lax.dot_general(rows, grad, (((0,), (0,)), ((), ())), preferred_element_type=jnp.float32).astype(
            jnp.bfloat16
        )
        copies.append(pltpu.make_async_copy(held.at[k], out_ref.at[pl.ds(k * step, step)], sems.at[k]))
        copies[-1].start()
    loss = cross / totals[0:1] - norms[0:1] + norms[1:2] + CE_WEIGHT * (norms[1:2] - label_logit)
    mine = lax.broadcasted_iota(jnp.int32, (count, count), 0) + me * rows_local == lanes
    by_lane = lax.broadcasted_iota(jnp.int32, (count, count), 0) == lanes
    loss_out[...] = jnp.sum(jnp.where(by_lane, to_column(mine, loss), 0.0), axis=0, keepdims=True)
    for copy in copies:
        copy.wait()


def head_gradient(me, label, stats, logits, hidden, depth, rows_local, tuned):
    count, vocab = logits[0].shape
    step = min(256, depth)
    vmem = pl.BlockSpec(memory_space=pltpu.VMEM)
    return pl.pallas_call(
        functools.partial(head_kernel, rows_local, tuned),
        in_specs=[pl.BlockSpec(memory_space=pltpu.SMEM)] + [vmem] * (4 + len(hidden)),
        out_specs=(pl.BlockSpec(memory_space=pltpu.HBM), vmem),
        out_shape=(jax.ShapeDtypeStruct((depth, vocab), jnp.bfloat16), jax.ShapeDtypeStruct((1, count), jnp.float32)),
        scratch_shapes=[
            pltpu.VMEM((depth // step, step, vocab), jnp.bfloat16),
            pltpu.SemaphoreType.DMA((depth // step,)),
        ],
        compiler_params=pltpu.CompilerParams(vmem_limit_bytes=VMEM_LIMIT),
        cost_estimate=pl.CostEstimate(
            flops=2 * count * depth * vocab, bytes_accessed=2 * depth * (vocab + count), transcendentals=2 * count * vocab
        ),
    )(me, label, stats, *logits, *hidden)


def swap(value, distance, n):
    return lax.ppermute(value, "dp", [(i, i ^ distance) for i in range(n)])


def after(value, *done):
    return lax.optimization_barrier((value, *done))[0]


def join_kernel(teacher_ref, student_ref, out_ref, sems):
    depth = teacher_ref.shape[1]
    copies = [
        pltpu.make_async_copy(ref, out_ref.at[:, pl.ds(j * depth, depth)], sems.at[j])
        for j, ref in enumerate((teacher_ref, student_ref))
    ]
    for copy in copies:
        copy.start()
    for copy in copies:
        copy.wait()


def join_rows(teacher_rows, student_rows):
    count, depth = teacher_rows.shape
    return pl.pallas_call(
        join_kernel,
        in_specs=[pl.BlockSpec(memory_space=pltpu.HBM)] * 2,
        out_specs=pl.BlockSpec(memory_space=pltpu.VMEM),
        out_shape=jax.ShapeDtypeStruct((count, 2 * depth), teacher_rows.dtype),
        scratch_shapes=[pltpu.SemaphoreType.DMA((2,))],
        compiler_params=pltpu.CompilerParams(vmem_limit_bytes=2**20),
        cost_estimate=pl.CostEstimate(flops=0, bytes_accessed=8 * count * depth, transcendentals=0),
    )(stay(teacher_rows), stay(student_rows))


def gather_rows(teacher_rows, student_rows, n, fetch):
    join = lambda pair: jnp.concatenate(pair, axis=1)
    stack = lambda *parts: jnp.concatenate(parts, axis=0)
    depth = teacher_rows.shape[1]
    far_teacher = swap(teacher_rows, 8, n)
    rows = join_rows(teacher_rows, student_rows)
    far_student = swap(student_rows, 8, n)
    near, side = swap(rows, 4, n), swap(rows, 2, n)
    fetched = fetch(rows)
    far = join((far_teacher, far_student))
    far_ready = after(far, *fetched)
    near_ready = near
    far, near = far_ready, near_ready
    far_near = swap(far, 4, n)
    *fetched, turned = fetched
    other_head = swap(after(turned, far, near), 1, n)
    far_side = swap(far, 2, n)
    near_side = swap(near, 2, n)
    far_near_side = swap(far_near, 2, n)
    held = [stack(rows, side, near, near_side), stack(far, far_side, far_near, far_near_side)]
    return held + [swap(piece, 1, n) for piece in held], fetched, (turned, other_head)


def scatter_rows(near_keep, near_send, far_keep, far_send, rows_local, n, head_gradient_of):
    low = jnp.bfloat16
    full = jnp.float32
    far_other = swap(far_send, 2, n)
    grad_head, loss = head_gradient_of(far_send)
    near_other = swap(after(near_send, grad_head), 2, n)
    far = (far_keep + far_other.astype(full)).astype(low)
    from_far = swap(far[:rows_local], 8, n)
    from_far_near = swap(far[rows_local:], 12, n)
    near = near_keep + near_other.astype(full)
    from_near = swap(near[rows_local:].astype(low), 4, n)
    total = near[:rows_local] + from_far.astype(full) + from_far_near.astype(full) + from_near.astype(full)
    return total, grad_head, loss


def per_device(n, teacher_hidden, student_hidden, teacher_head, student_head, labels, order):
    rows_local, depth = student_hidden.shape
    tuned = n == 16 and rows_local == 8
    me = lax.axis_index("dp").astype(jnp.int32).reshape(1)
    heads = (teacher_head, student_head)
    fetch = lambda *done: prepare(after(me, *done), order, labels, heads, rows_local, tuned)
    if tuned:
        hidden, fetched, turned = gather_rows(teacher_hidden, student_hidden, n, fetch)
    else:
        fetched = fetch(me)
        rows = jnp.concatenate([teacher_hidden, student_hidden], axis=1)
        hidden = [lax.all_gather(rows, "dp", axis=0, tiled=True)]
    *heads, pick, label = fetched
    *logit, stats = logits(me, pick, label, hidden, heads, n, rows_local, tuned)
    if tuned:
        stats, away = logit.pop(), swap(stats, 1, n)
    stats = lax.all_to_all(stats, "dp", 0, 0)
    head_gradient_of = lambda *done: head_gradient(after(me, *done), label, stats, logit, hidden, depth, rows_local, tuned)
    if tuned:
        parts = gradient(me, label, stats, (*logit, away), turned, rows_local, tuned)
        grad_hidden, grad_head, loss = scatter_rows(*parts, rows_local, n, head_gradient_of)
    else:
        (part,) = gradient(me, label, stats, logit, heads[1:], rows_local, tuned)
        grad_head, loss = head_gradient_of()
        grad_hidden = lax.psum_scatter(part, "dp", scatter_dimension=0, tiled=True)
    return (loss[0, :rows_local], grad_hidden, grad_head)


def solution(mesh):
    in_specs = (
        P(("groups", "dp"), None),
        P(("groups", "dp"), None),
        P(None, "dp"),
        P(None, "dp"),
        P("groups"),
        P("groups"),
    )
    out_specs = (P(("groups", "dp")), P(("groups", "dp"), None), P("groups", "dp"))
    return jax.shard_map(
        functools.partial(per_device, mesh.shape["dp"]),
        mesh=mesh,
        in_specs=in_specs,
        out_specs=out_specs,
        check_vma=False,
    )
```

```python
import functools

import jax
import jax.numpy as jnp
from jax import lax
from jax.experimental import pallas as pl
from jax.experimental.pallas import tpu as pltpu
from jax.sharding import PartitionSpec as P

CE_WEIGHT = 0.5
VMEM_LIMIT = 28 * 2**20
STATS = 8


def held_rows(shape, dim, me, rows_local, tuned):
    held = lax.broadcasted_iota(jnp.int32, shape, dim)
    if not tuned:
        return held
    step = rows_local.bit_length() - 1
    block = lax.shift_right_logical(held, step)
    distance = (block & 7) * 2 + lax.shift_right_logical(block, 3)
    return (me ^ distance) * rows_local + (held & (rows_local - 1))


def to_column(is_row, row):
    return jnp.sum(jnp.where(is_row, row, 0.0), axis=1, keepdims=True)


def prepare_kernel(rows_local, tuned, me_ref, order_ref, labels_ref, *refs):
    teacher_ref, student_ref, teacher_out, student_out, pick_out, label_out, *turned_out = refs[: -4]
    ids, id_sems, teacher_sem, student_sems = refs[-4:]
    id_copies = [
        pltpu.make_async_copy(source, ids.at[j], id_sems.at[j]) for j, source in enumerate((order_ref, labels_ref))
    ]
    pieces = student_sems.shape[0]
    rows = student_ref.shape[0] // pieces
    parts = [pl.ds(k * rows, rows) for k in range(pieces)]
    copies = [
        pltpu.make_async_copy(student_ref.at[part], student_out.at[part], student_sems.at[k])
        for k, part in enumerate(parts)
    ]
    copies.append(pltpu.make_async_copy(teacher_ref, teacher_out, teacher_sem))
    for copy in id_copies + copies:
        copy.start()
    me = me_ref[0]
    count = order_ref.shape[1]
    vocab = teacher_ref.shape[1]
    lanes = lax.broadcasted_iota(jnp.int32, (count, count), 1)
    is_row = held_rows((count, count), 0, me, rows_local, tuned) == lanes
    have = held_rows((count, count), 1, me, rows_local, tuned).astype(jnp.float32)
    for copy in id_copies:
        copy.wait()
    wanted = to_column(is_row, ids[0].astype(jnp.float32))
    pick_out[...] = jnp.where(wanted == have, 1.0, 0.0).astype(jnp.bfloat16)
    label = to_column(is_row, ids[1].astype(jnp.float32)) - (me * vocab).astype(jnp.float32)
    label_out[...] = jnp.broadcast_to(label, label_out.shape)
    for k, copy in enumerate(copies):
        copy.wait()
        if k < pieces:
            for out in turned_out:
                out[:, k * rows : (k + 1) * rows] = student_out[k * rows : (k + 1) * rows].T


def stay(value):
    return pltpu.with_memory_space_constraint(value, pltpu.HBM)


def prepare(me, order, labels, heads, rows_local, tuned):
    count = order.shape[0]
    vmem = pl.BlockSpec(memory_space=pltpu.VMEM)
    hbm = pl.BlockSpec(memory_space=pltpu.HBM)
    shapes = [
        jax.ShapeDtypeStruct(heads[0].shape, heads[0].dtype),
        jax.ShapeDtypeStruct(heads[1].shape, heads[1].dtype),
        jax.ShapeDtypeStruct((count, count), jnp.bfloat16),
        jax.ShapeDtypeStruct((count, 128), jnp.float32),
    ] + [jax.ShapeDtypeStruct(heads[1].shape[::-1], heads[1].dtype)] * tuned
    return pl.pallas_call(
        functools.partial(prepare_kernel, rows_local, tuned),
        in_specs=[pl.BlockSpec(memory_space=pltpu.SMEM)] + [hbm] * 4,
        out_specs=(vmem,) * len(shapes),
        out_shape=tuple(shapes),
        scratch_shapes=[
            pltpu.VMEM((2, 1, count), jnp.int32),
            pltpu.SemaphoreType.DMA((2,)),
            pltpu.SemaphoreType.DMA,
            pltpu.SemaphoreType.DMA((8,)),
        ],
        compiler_params=pltpu.CompilerParams(vmem_limit_bytes=24 * 2**20),
        cost_estimate=pl.CostEstimate(flops=0, bytes_accessed=heads[0].size * 8, transcendentals=0),
    )(me, stay(order[None]), stay(labels[None]), *map(stay, heads))


def logits_kernel(rows_local, tuned, parts, me_ref, pick_ref, label_ref, *refs):
    pieces = refs[:parts]
    teacher_head, student_head, teacher_out, student_out, stats_out, *away_out = refs[parts:]
    depth, vocab = student_head.shape

    def product(first, head):
        rows = jnp.concatenate([piece[:, first : first + depth] for piece in pieces], axis=0)
        return jnp.dot(rows, head[...], preferred_element_type=jnp.float32)

    me = me_ref[0]
    raw = product(0, teacher_head)
    student = product(depth, student_head)
    count = student.shape[0]
    high = raw.astype(jnp.bfloat16)
    rest = raw - high.astype(jnp.float32)
    middle = rest.astype(jnp.bfloat16)
    low = (rest - middle.astype(jnp.float32)).astype(jnp.bfloat16)
    pick = pick_ref[...]
    teacher = sum(jnp.dot(pick, piece, preferred_element_type=jnp.float32) for piece in (high, middle, low))
    teacher_out[...] = teacher
    student_out[...] = student
    for out in away_out:
        out[0] = teacher[count // 2 :]
        out[1] = student[count // 2 :]
    is_label = label_ref[:, 0:1].astype(jnp.int32) == lax.broadcasted_iota(jnp.int32, (count, vocab), 1)
    teacher_max = jnp.max(teacher, axis=1, keepdims=True)
    student_max = jnp.max(student, axis=1, keepdims=True)
    teacher_exp = jnp.exp(teacher - teacher_max)
    values = (
        teacher_max,
        student_max,
        jnp.sum(teacher_exp, axis=1, keepdims=True),
        jnp.sum(jnp.exp(student - student_max), axis=1, keepdims=True),
        jnp.sum(teacher_exp * (teacher - student), axis=1, keepdims=True),
        jnp.sum(jnp.where(is_label, student, 0.0), axis=1, keepdims=True),
    )
    lanes = lax.broadcasted_iota(jnp.int32, (count, count), 1)
    is_row = held_rows((count, count), 0, me, rows_local, tuned) == lanes
    block = [jnp.sum(jnp.where(is_row, value, 0.0), axis=0, keepdims=True) for value in values]
    block.append(jnp.zeros((STATS - len(block), count), jnp.float32))
    stats_out[...] = jnp.broadcast_to(jnp.concatenate(block, axis=0)[None], stats_out.shape)


def logits(me, pick, label, hidden, heads, n, rows_local, tuned):
    count = pick.shape[0]
    depth, vocab = heads[0].shape
    vmem = pl.BlockSpec(memory_space=pltpu.VMEM)
    shapes = [(count, vocab), (count, vocab), (n, STATS, count)] + [(2, count // 2, vocab)] * tuned
    return pl.pallas_call(
        functools.partial(logits_kernel, rows_local, tuned, len(hidden)),
        in_specs=[pl.BlockSpec(memory_space=pltpu.SMEM)] + [vmem] * (4 + len(hidden)),
        out_specs=(vmem,) * len(shapes),
        out_shape=tuple(jax.ShapeDtypeStruct(shape, jnp.float32) for shape in shapes),
        compiler_params=pltpu.CompilerParams(vmem_limit_bytes=VMEM_LIMIT),
        cost_estimate=pl.CostEstimate(
            flops=4 * count * depth * vocab, bytes_accessed=4 * depth * (vocab + count), transcendentals=2 * count * vocab
        ),
    )(me, pick, label, *hidden, *heads)


def merged(stats_ref):
    devices, _, count = stats_ref.shape
    top = stats_ref[0, 0:2]
    for d in range(1, devices):
        top = jnp.maximum(top, stats_ref[d, 0:2])
    totals = jnp.zeros((2, count), jnp.float32)
    cross = jnp.zeros((1, count), jnp.float32)
    label_logit = jnp.zeros((1, count), jnp.float32)
    for d in range(devices):
        weight = jnp.exp(stats_ref[d, 0:2] - top)
        totals += weight * stats_ref[d, 2:4]
        cross += weight[0:1] * stats_ref[d, 4:5]
        label_logit += stats_ref[d, 5:6]
    return top + jnp.log(totals), totals, cross, label_logit


def logit_gradient(teacher, student, norms, is_row, label):
    is_label = label.astype(jnp.int32) == lax.broadcasted_iota(jnp.int32, student.shape, 1)
    return (
        (1.0 + CE_WEIGHT) * jnp.exp(student - to_column(is_row, norms[1:2]))
        - jnp.exp(teacher - to_column(is_row, norms[0:1]))
        - jnp.where(is_label, CE_WEIGHT, 0.0)
    ).astype(jnp.bfloat16)


def times_transposed(grad, head):
    return lax.dot_general(grad, head, (((1,), (1,)), ((), ())), preferred_element_type=jnp.float32)


def grad_kernel(
    rows_local, me_ref, label_ref, stats_ref, teacher_ref, student_ref, away_ref, turned_ref, other_ref, *outs
):
    near_keep, near_send, far_keep, far_send = outs
    me = me_ref[0]
    count, vocab = student_ref.shape
    own = count // 2
    norms = merged(stats_ref)[0]
    is_row = held_rows((own, count), 0, me, rows_local, True) == lax.broadcasted_iota(jnp.int32, (own, count), 1)
    label = label_ref[:own, 0:1]
    grad = logit_gradient(teacher_ref[:own], student_ref[:own], norms, is_row, label)
    shift = jnp.where((me & 1) == 0, -vocab, vocab).astype(jnp.float32)
    other = logit_gradient(away_ref[0], away_ref[1], norms, is_row, label + shift)
    depth = turned_ref.shape[1]
    step = min(512, depth)
    for k in range(0, depth, step):
        part = jnp.dot(grad, turned_ref[:, k : k + step], preferred_element_type=jnp.float32)
        part += jnp.dot(other, other_ref[:, k : k + step], preferred_element_type=jnp.float32)
        blocks = [part[b * rows_local : (b + 1) * rows_local] for b in range(8)]
        for j, out in enumerate((near_keep, near_send, far_keep, far_send)):
            first = (j // 2) * 4 + j % 2
            out[:, k : k + step] = jnp.concatenate((blocks[first], blocks[first + 2]), axis=0).astype(out.dtype)


def whole_grad_kernel(rows_local, me_ref, label_ref, stats_ref, teacher_ref, student_ref, head_ref, out_ref):
    count, vocab = student_ref.shape
    norms = merged(stats_ref)[0]
    is_row = held_rows((count, count), 0, me_ref[0], rows_local, False) == lax.broadcasted_iota(
        jnp.int32, (count, count), 1
    )
    grad = logit_gradient(teacher_ref[...], student_ref[...], norms, is_row, label_ref[:, 0:1])
    depth = head_ref.shape[0]
    step = min(512, depth)
    for k in range(0, depth, step):
        out_ref[:, k : k + step] = times_transposed(grad, head_ref[k : k + step])


def gradient(me, label, stats, logits, heads, rows_local, tuned):
    count, vocab = logits[0].shape
    depth = heads[0].shape[1 if tuned else 0]
    vmem = pl.BlockSpec(memory_space=pltpu.VMEM)
    if tuned:
        shapes = [jax.ShapeDtypeStruct((2 * rows_local, depth), kind) for kind in (jnp.float32, jnp.bfloat16)] * 2
    else:
        shapes = [jax.ShapeDtypeStruct((count, depth), jnp.float32)]
    return pl.pallas_call(
        functools.partial(grad_kernel if tuned else whole_grad_kernel, rows_local),
        in_specs=[pl.BlockSpec(memory_space=pltpu.SMEM)] + [vmem] * (2 + len(logits) + len(heads)),
        out_specs=(vmem,) * len(shapes),
        out_shape=tuple(shapes),
        compiler_params=pltpu.CompilerParams(vmem_limit_bytes=VMEM_LIMIT),
        cost_estimate=pl.CostEstimate(
            flops=2 * count * depth * vocab, bytes_accessed=2 * depth * (vocab + 2 * count), transcendentals=2 * count * vocab
        ),
    )(me, label, stats, *logits, *heads)


def head_kernel(rows_local, tuned, me_ref, label_ref, stats_ref, teacher_ref, student_ref, *refs):
    *pieces, out_ref, loss_out, held, sems = refs
    me = me_ref[0]
    count = student_ref.shape[0]
    lanes = lax.broadcasted_iota(jnp.int32, (count, count), 1)
    is_row = held_rows((count, count), 0, me, rows_local, tuned) == lanes
    norms, totals, cross, label_logit = merged(stats_ref)
    grad = logit_gradient(teacher_ref[...], student_ref[...], norms, is_row, label_ref[:, 0:1])
    steps, step, _ = held.shape
    copies = []
    for k in range(steps):
        first = (steps + k) * step
        rows = jnp.concatenate([piece[:, first : first + step] for piece in pieces], axis=0)
        held[k] = lax.dot_general(rows, grad, (((0,), (0,)), ((), ())), preferred_element_type=jnp.float32).astype(
            jnp.bfloat16
        )
        copies.append(pltpu.make_async_copy(held.at[k], out_ref.at[pl.ds(k * step, step)], sems.at[k]))
        copies[-1].start()
    loss = cross / totals[0:1] - norms[0:1] + norms[1:2] + CE_WEIGHT * (norms[1:2] - label_logit)
    mine = lax.broadcasted_iota(jnp.int32, (count, count), 0) + me * rows_local == lanes
    by_lane = lax.broadcasted_iota(jnp.int32, (count, count), 0) == lanes
    loss_out[...] = jnp.sum(jnp.where(by_lane, to_column(mine, loss), 0.0), axis=0, keepdims=True)
    for copy in copies:
        copy.wait()


def head_gradient(me, label, stats, logits, hidden, depth, rows_local, tuned):
    count, vocab = logits[0].shape
    step = min(256, depth)
    vmem = pl.BlockSpec(memory_space=pltpu.VMEM)
    return pl.pallas_call(
        functools.partial(head_kernel, rows_local, tuned),
        in_specs=[pl.BlockSpec(memory_space=pltpu.SMEM)] + [vmem] * (4 + len(hidden)),
        out_specs=(pl.BlockSpec(memory_space=pltpu.HBM), vmem),
        out_shape=(jax.ShapeDtypeStruct((depth, vocab), jnp.bfloat16), jax.ShapeDtypeStruct((1, count), jnp.float32)),
        scratch_shapes=[
            pltpu.VMEM((depth // step, step, vocab), jnp.bfloat16),
            pltpu.SemaphoreType.DMA((depth // step,)),
        ],
        compiler_params=pltpu.CompilerParams(vmem_limit_bytes=VMEM_LIMIT),
        cost_estimate=pl.CostEstimate(
            flops=2 * count * depth * vocab, bytes_accessed=2 * depth * (vocab + count), transcendentals=2 * count * vocab
        ),
    )(me, label, stats, *logits, *hidden)


def swap(value, distance, n):
    return lax.ppermute(value, "dp", [(i, i ^ distance) for i in range(n)])


def after(value, *done):
    return lax.optimization_barrier((value, *done))[0]


def join_kernel(teacher_ref, student_ref, out_ref, sems):
    depth = teacher_ref.shape[1]
    copies = [
        pltpu.make_async_copy(ref, out_ref.at[:, pl.ds(j * depth, depth)], sems.at[j])
        for j, ref in enumerate((teacher_ref, student_ref))
    ]
    for copy in copies:
        copy.start()
    for copy in copies:
        copy.wait()


def join_rows(teacher_rows, student_rows):
    count, depth = teacher_rows.shape
    return pl.pallas_call(
        join_kernel,
        in_specs=[pl.BlockSpec(memory_space=pltpu.HBM)] * 2,
        out_specs=pl.BlockSpec(memory_space=pltpu.VMEM),
        out_shape=jax.ShapeDtypeStruct((count, 2 * depth), teacher_rows.dtype),
        scratch_shapes=[pltpu.SemaphoreType.DMA((2,))],
        compiler_params=pltpu.CompilerParams(vmem_limit_bytes=2**20),
        cost_estimate=pl.CostEstimate(flops=0, bytes_accessed=8 * count * depth, transcendentals=0),
    )(stay(teacher_rows), stay(student_rows))


def gather_rows(teacher_rows, student_rows, n, fetch):
    join = lambda pair: jnp.concatenate(pair, axis=1)
    stack = lambda *parts: jnp.concatenate(parts, axis=0)
    far_teacher = swap(teacher_rows, 8, n)
    rows = join_rows(teacher_rows, student_rows)
    far_student = swap(student_rows, 8, n)
    near, side = swap(rows, 4, n), swap(rows, 2, n)
    *fetched, turned = fetch(rows)
    far = after(join((far_teacher, far_student)), *fetched, turned)
    far_near = swap(far, 4, n)
    other_head = swap(after(turned, far), 1, n)
    far_side = swap(far, 2, n)
    near_side = swap(side, 4, n)
    far_near_side = swap(far_near, 2, n)
    held = [stack(rows, side, near, near_side, far, far_side), stack(far_near, far_near_side)]
    return held + [swap(piece, 1, n) for piece in held], fetched, (turned, other_head)


def scatter_rows(near_keep, near_send, far_keep, far_send, rows_local, n, head_gradient_of):
    low = jnp.bfloat16
    full = jnp.float32
    far_other = swap(far_send, 2, n)
    grad_head, loss = head_gradient_of(far_send)
    near_other = swap(after(near_send, grad_head), 2, n)
    far = (far_keep + far_other.astype(full)).astype(low)
    from_far = swap(far[:rows_local], 8, n)
    from_far_near = swap(far[rows_local:], 12, n)
    near = near_keep + near_other.astype(full)
    from_near = swap(near[rows_local:].astype(low), 4, n)
    total = near[:rows_local] + from_far.astype(full) + from_far_near.astype(full) + from_near.astype(full)
    return total, grad_head, loss


def per_device(n, teacher_hidden, student_hidden, teacher_head, student_head, labels, order):
    rows_local, depth = student_hidden.shape
    tuned = n == 16 and rows_local == 8
    me = lax.axis_index("dp").astype(jnp.int32).reshape(1)
    heads = (teacher_head, student_head)
    fetch = lambda *done: prepare(after(me, *done), order, labels, heads, rows_local, tuned)
    if tuned:
        hidden, fetched, turned = gather_rows(teacher_hidden, student_hidden, n, fetch)
    else:
        fetched = fetch(me)
        rows = jnp.concatenate([teacher_hidden, student_hidden], axis=1)
        hidden = [lax.all_gather(rows, "dp", axis=0, tiled=True)]
    *heads, pick, label = fetched
    *logit, stats = logits(me, pick, label, hidden, heads, n, rows_local, tuned)
    if tuned:
        stats, away = logit.pop(), swap(stats, 1, n)
    stats = lax.all_to_all(stats, "dp", 0, 0)
    head_gradient_of = lambda *done: head_gradient(after(me, *done), label, stats, logit, hidden, depth, rows_local, tuned)
    if tuned:
        parts = gradient(me, label, stats, (*logit, away), turned, rows_local, tuned)
        grad_hidden, grad_head, loss = scatter_rows(*parts, rows_local, n, head_gradient_of)
    else:
        (part,) = gradient(me, label, stats, logit, heads[1:], rows_local, tuned)
        grad_head, loss = head_gradient_of()
        grad_hidden = lax.psum_scatter(part, "dp", scatter_dimension=0, tiled=True)
    return (loss[0, :rows_local], grad_hidden, grad_head)


def solution(mesh):
    in_specs = (
        P(("groups", "dp"), None),
        P(("groups", "dp"), None),
        P(None, "dp"),
        P(None, "dp"),
        P("groups"),
        P("groups"),
    )
    out_specs = (P(("groups", "dp")), P(("groups", "dp"), None), P("groups", "dp"))
    return jax.shard_map(
        functools.partial(per_device, mesh.shape["dp"]),
        mesh=mesh,
        in_specs=in_specs,
        out_specs=out_specs,
        check_vma=False,
    )
```

```python
import functools

import jax
import jax.numpy as jnp
from jax import lax
from jax.experimental import pallas as pl
from jax.experimental.pallas import tpu as pltpu
from jax.sharding import PartitionSpec as P

CE_WEIGHT = 0.5
VMEM_LIMIT = 28 * 2**20
STATS = 4


def held_rows(shape, dim, me, rows_local, tuned):
    held = lax.broadcasted_iota(jnp.int32, shape, dim)
    if not tuned:
        return held
    step = rows_local.bit_length() - 1
    block = lax.shift_right_logical(held, step)
    distance = (block & 7) * 2 + lax.shift_right_logical(block, 3)
    return (me ^ distance) * rows_local + (held & (rows_local - 1))


def to_column(is_row, row):
    return jnp.sum(jnp.where(is_row, row, 0.0), axis=1, keepdims=True)


def prepare_kernel(rows_local, tuned, me_ref, order_ref, labels_ref, *refs):
    teacher_ref, student_ref, teacher_out, student_out, pick_out, label_out, *turned_out = refs[: -4]
    ids, id_sems, teacher_sem, student_sems = refs[-4:]
    id_copies = [
        pltpu.make_async_copy(source, ids.at[j], id_sems.at[j]) for j, source in enumerate((order_ref, labels_ref))
    ]
    pieces = student_sems.shape[0]
    rows = student_ref.shape[0] // pieces
    parts = [pl.ds(k * rows, rows) for k in range(pieces)]
    copies = [
        pltpu.make_async_copy(student_ref.at[part], student_out.at[part], student_sems.at[k])
        for k, part in enumerate(parts)
    ]
    copies.append(pltpu.make_async_copy(teacher_ref, teacher_out, teacher_sem))
    for copy in id_copies + copies:
        copy.start()
    me = me_ref[0]
    count = order_ref.shape[1]
    vocab = teacher_ref.shape[1]
    lanes = lax.broadcasted_iota(jnp.int32, (count, count), 1)
    is_row = held_rows((count, count), 0, me, rows_local, tuned) == lanes
    have = held_rows((count, count), 1, me, rows_local, tuned).astype(jnp.float32)
    for copy in id_copies:
        copy.wait()
    wanted = to_column(is_row, ids[0].astype(jnp.float32))
    pick_out[...] = jnp.where(wanted == have, 1.0, 0.0).astype(jnp.bfloat16)
    label = to_column(is_row, ids[1].astype(jnp.float32)) - (me * vocab).astype(jnp.float32)
    label_out[...] = jnp.broadcast_to(label, label_out.shape)
    for k, copy in enumerate(copies):
        copy.wait()
        if k < pieces:
            for out in turned_out:
                out[:, k * rows : (k + 1) * rows] = student_out[k * rows : (k + 1) * rows].T


def stay(value):
    return pltpu.with_memory_space_constraint(value, pltpu.HBM)


def prepare(me, order, labels, heads, rows_local, tuned):
    count = order.shape[0]
    vmem = pl.BlockSpec(memory_space=pltpu.VMEM)
    hbm = pl.BlockSpec(memory_space=pltpu.HBM)
    shapes = [
        jax.ShapeDtypeStruct(heads[0].shape, heads[0].dtype),
        jax.ShapeDtypeStruct(heads[1].shape, heads[1].dtype),
        jax.ShapeDtypeStruct((count, count), jnp.bfloat16),
        jax.ShapeDtypeStruct((count, 128), jnp.float32),
    ] + [jax.ShapeDtypeStruct(heads[1].shape[::-1], heads[1].dtype)] * tuned
    return pl.pallas_call(
        functools.partial(prepare_kernel, rows_local, tuned),
        in_specs=[pl.BlockSpec(memory_space=pltpu.SMEM)] + [hbm] * 4,
        out_specs=(vmem,) * len(shapes),
        out_shape=tuple(shapes),
        scratch_shapes=[
            pltpu.VMEM((2, 1, count), jnp.int32),
            pltpu.SemaphoreType.DMA((2,)),
            pltpu.SemaphoreType.DMA,
            pltpu.SemaphoreType.DMA((8,)),
        ],
        compiler_params=pltpu.CompilerParams(vmem_limit_bytes=24 * 2**20),
        cost_estimate=pl.CostEstimate(flops=0, bytes_accessed=heads[0].size * 8, transcendentals=0),
    )(me, stay(order[None]), stay(labels[None]), *map(stay, heads))


def logits_kernel(rows_local, tuned, parts, me_ref, pick_ref, label_ref, *refs):
    pieces = refs[:parts]
    teacher_head, student_head, teacher_out, student_out, stats_out, *away_out = refs[parts:]
    depth, vocab = student_head.shape

    def product(first, head):
        rows = jnp.concatenate([piece[:, first : first + depth] for piece in pieces], axis=0)
        return jnp.dot(rows, head[...], preferred_element_type=jnp.float32)

    me = me_ref[0]
    raw = product(0, teacher_head)
    student = product(depth, student_head)
    count = student.shape[0]
    high = raw.astype(jnp.bfloat16)
    rest = raw - high.astype(jnp.float32)
    middle = rest.astype(jnp.bfloat16)
    low = (rest - middle.astype(jnp.float32)).astype(jnp.bfloat16)
    pick = pick_ref[...]
    teacher = sum(jnp.dot(pick, piece, preferred_element_type=jnp.float32) for piece in (high, middle, low))
    teacher_out[...] = teacher
    student_out[...] = student
    for out in away_out:
        out[0] = teacher[count // 2 :]
        out[1] = student[count // 2 :]
    is_label = label_ref[:, 0:1].astype(jnp.int32) == lax.broadcasted_iota(jnp.int32, (count, vocab), 1)
    teacher_max = jnp.max(teacher, axis=1, keepdims=True)
    student_max = jnp.max(student, axis=1, keepdims=True)
    teacher_exp = jnp.exp(teacher - teacher_max)
    teacher_total = jnp.sum(teacher_exp, axis=1, keepdims=True)
    student_total = jnp.sum(jnp.exp(student - student_max), axis=1, keepdims=True)
    values = (
        teacher_max + jnp.log(teacher_total),
        student_max + jnp.log(student_total),
        jnp.sum(teacher_exp * (teacher - student), axis=1, keepdims=True) / teacher_total,
        jnp.sum(jnp.where(is_label, student, 0.0), axis=1, keepdims=True),
    )
    lanes = lax.broadcasted_iota(jnp.int32, (count, count), 1)
    is_row = held_rows((count, count), 0, me, rows_local, tuned) == lanes
    block = [jnp.sum(jnp.where(is_row, value, 0.0), axis=0, keepdims=True) for value in values]
    stats_out[...] = jnp.broadcast_to(jnp.concatenate(block, axis=0)[None], stats_out.shape)


def logits(me, pick, label, hidden, heads, n, rows_local, tuned):
    count = pick.shape[0]
    depth, vocab = heads[0].shape
    vmem = pl.BlockSpec(memory_space=pltpu.VMEM)
    shapes = [(count, vocab), (count, vocab), (n, STATS, count)] + [(2, count // 2, vocab)] * tuned
    return pl.pallas_call(
        functools.partial(logits_kernel, rows_local, tuned, len(hidden)),
        in_specs=[pl.BlockSpec(memory_space=pltpu.SMEM)] + [vmem] * (4 + len(hidden)),
        out_specs=(vmem,) * len(shapes),
        out_shape=tuple(jax.ShapeDtypeStruct(shape, jnp.float32) for shape in shapes),
        compiler_params=pltpu.CompilerParams(vmem_limit_bytes=VMEM_LIMIT),
        cost_estimate=pl.CostEstimate(
            flops=4 * count * depth * vocab, bytes_accessed=4 * depth * (vocab + count), transcendentals=2 * count * vocab
        ),
    )(me, pick, label, *hidden, *heads)


def merged(stats_ref):
    devices, _, count = stats_ref.shape
    top = stats_ref[0, 0:2]
    for d in range(1, devices):
        top = jnp.maximum(top, stats_ref[d, 0:2])
    totals = jnp.zeros((2, count), jnp.float32)
    cross = jnp.zeros((1, count), jnp.float32)
    label_logit = jnp.zeros((1, count), jnp.float32)
    for d in range(devices):
        weight = jnp.exp(stats_ref[d, 0:2] - top)
        totals += weight
        cross += weight[0:1] * stats_ref[d, 2:3]
        label_logit += stats_ref[d, 3:4]
    return top + jnp.log(totals), cross / totals[0:1], label_logit


def logit_gradient(teacher, student, norms, is_row, label):
    is_label = label.astype(jnp.int32) == lax.broadcasted_iota(jnp.int32, student.shape, 1)
    return (
        (1.0 + CE_WEIGHT) * jnp.exp(student - to_column(is_row, norms[1:2]))
        - jnp.exp(teacher - to_column(is_row, norms[0:1]))
        - jnp.where(is_label, CE_WEIGHT, 0.0)
    ).astype(jnp.bfloat16)


def times_transposed(grad, head):
    return lax.dot_general(grad, head, (((1,), (1,)), ((), ())), preferred_element_type=jnp.float32)


def grad_kernel(
    rows_local, me_ref, label_ref, stats_ref, teacher_ref, student_ref, away_ref, turned_ref, other_ref, *outs
):
    near_keep, near_send, far_keep, far_send = outs
    me = me_ref[0]
    count, vocab = student_ref.shape
    own = count // 2
    norms = merged(stats_ref)[0]
    is_row = held_rows((own, count), 0, me, rows_local, True) == lax.broadcasted_iota(jnp.int32, (own, count), 1)
    label = label_ref[:own, 0:1]
    grad = logit_gradient(teacher_ref[:own], student_ref[:own], norms, is_row, label)
    shift = jnp.where((me & 1) == 0, -vocab, vocab).astype(jnp.float32)
    other = logit_gradient(away_ref[0], away_ref[1], norms, is_row, label + shift)
    depth = turned_ref.shape[1]
    step = min(512, depth)
    for k in range(0, depth, step):
        part = jnp.dot(grad, turned_ref[:, k : k + step], preferred_element_type=jnp.float32)
        part += jnp.dot(other, other_ref[:, k : k + step], preferred_element_type=jnp.float32)
        blocks = [part[b * rows_local : (b + 1) * rows_local] for b in range(8)]
        for out, first, second in ((near_keep, 0, 1), (near_send, 2, 3), (far_keep, 4, 6), (far_send, 5, 7)):
            out[:, k : k + step] = jnp.concatenate((blocks[first], blocks[second]), axis=0).astype(out.dtype)


def whole_grad_kernel(rows_local, me_ref, label_ref, stats_ref, teacher_ref, student_ref, head_ref, out_ref):
    count, vocab = student_ref.shape
    norms = merged(stats_ref)[0]
    is_row = held_rows((count, count), 0, me_ref[0], rows_local, False) == lax.broadcasted_iota(
        jnp.int32, (count, count), 1
    )
    grad = logit_gradient(teacher_ref[...], student_ref[...], norms, is_row, label_ref[:, 0:1])
    depth = head_ref.shape[0]
    step = min(512, depth)
    for k in range(0, depth, step):
        out_ref[:, k : k + step] = times_transposed(grad, head_ref[k : k + step])


def gradient(me, label, stats, logits, heads, rows_local, tuned):
    count, vocab = logits[0].shape
    depth = heads[0].shape[1 if tuned else 0]
    vmem = pl.BlockSpec(memory_space=pltpu.VMEM)
    if tuned:
        shapes = [jax.ShapeDtypeStruct((2 * rows_local, depth), kind) for kind in (jnp.float32, jnp.bfloat16)] * 2
    else:
        shapes = [jax.ShapeDtypeStruct((count, depth), jnp.float32)]
    return pl.pallas_call(
        functools.partial(grad_kernel if tuned else whole_grad_kernel, rows_local),
        in_specs=[pl.BlockSpec(memory_space=pltpu.SMEM)] + [vmem] * (2 + len(logits) + len(heads)),
        out_specs=(vmem,) * len(shapes),
        out_shape=tuple(shapes),
        compiler_params=pltpu.CompilerParams(vmem_limit_bytes=VMEM_LIMIT),
        cost_estimate=pl.CostEstimate(
            flops=2 * count * depth * vocab, bytes_accessed=2 * depth * (vocab + 2 * count), transcendentals=2 * count * vocab
        ),
    )(me, label, stats, *logits, *heads)


def head_kernel(rows_local, tuned, me_ref, label_ref, stats_ref, teacher_ref, student_ref, *refs):
    *pieces, out_ref, held, sems = refs
    me = me_ref[0]
    count = student_ref.shape[0]
    lanes = lax.broadcasted_iota(jnp.int32, (count, count), 1)
    is_row = held_rows((count, count), 0, me, rows_local, tuned) == lanes
    norms = merged(stats_ref)[0]
    grad = logit_gradient(teacher_ref[...], student_ref[...], norms, is_row, label_ref[:, 0:1])
    steps, step, _ = held.shape
    copies = []
    for k in range(steps):
        first = (steps + k) * step
        rows = jnp.concatenate([piece[:, first : first + step] for piece in pieces], axis=0)
        held[k] = lax.dot_general(rows, grad, (((0,), (0,)), ((), ())), preferred_element_type=jnp.float32).astype(
            jnp.bfloat16
        )
        copies.append(pltpu.make_async_copy(held.at[k], out_ref.at[pl.ds(k * step, step)], sems.at[k]))
        copies[-1].start()
    for copy in copies:
        copy.wait()


def head_gradient(me, label, stats, logits, hidden, depth, rows_local, tuned):
    count, vocab = logits[0].shape
    step = min(256, depth)
    vmem = pl.BlockSpec(memory_space=pltpu.VMEM)
    return pl.pallas_call(
        functools.partial(head_kernel, rows_local, tuned),
        in_specs=[pl.BlockSpec(memory_space=pltpu.SMEM)] + [vmem] * (4 + len(hidden)),
        out_specs=pl.BlockSpec(memory_space=pltpu.HBM),
        out_shape=jax.ShapeDtypeStruct((depth, vocab), jnp.bfloat16),
        scratch_shapes=[
            pltpu.VMEM((depth // step, step, vocab), jnp.bfloat16),
            pltpu.SemaphoreType.DMA((depth // step,)),
        ],
        compiler_params=pltpu.CompilerParams(vmem_limit_bytes=VMEM_LIMIT),
        cost_estimate=pl.CostEstimate(
            flops=2 * count * depth * vocab, bytes_accessed=2 * depth * (vocab + count), transcendentals=2 * count * vocab
        ),
    )(me, label, stats, *logits, *hidden)


def loss_kernel(rows_local, me_ref, stats_ref, loss_out):
    count = stats_ref.shape[2]
    norms, cross, label_logit = merged(stats_ref)
    loss = cross - norms[0:1] + norms[1:2] + CE_WEIGHT * (norms[1:2] - label_logit)
    lanes = lax.broadcasted_iota(jnp.int32, (count, count), 1)
    mine = lax.broadcasted_iota(jnp.int32, (count, count), 0) + me_ref[0] * rows_local == lanes
    by_lane = lax.broadcasted_iota(jnp.int32, (count, count), 0) == lanes
    loss_out[...] = jnp.sum(jnp.where(by_lane, to_column(mine, loss), 0.0), axis=0, keepdims=True)


def row_loss(me, stats, rows_local):
    vmem = pl.BlockSpec(memory_space=pltpu.VMEM)
    return pl.pallas_call(
        functools.partial(loss_kernel, rows_local),
        in_specs=[pl.BlockSpec(memory_space=pltpu.SMEM), vmem],
        out_specs=vmem,
        out_shape=jax.ShapeDtypeStruct((1, stats.shape[2]), jnp.float32),
        compiler_params=pltpu.CompilerParams(vmem_limit_bytes=VMEM_LIMIT),
        cost_estimate=pl.CostEstimate(flops=0, bytes_accessed=stats.size * 4, transcendentals=stats.size // 4),
    )(me, stats)


def swap(value, distance, n):
    return lax.ppermute(value, "dp", [(i, i ^ distance) for i in range(n)])


def after(value, *done):
    return lax.optimization_barrier((value, *done))[0]


def join_kernel(teacher_ref, student_ref, out_ref, sems):
    depth = teacher_ref.shape[1]
    copies = [
        pltpu.make_async_copy(ref, out_ref.at[:, pl.ds(j * depth, depth)], sems.at[j])
        for j, ref in enumerate((teacher_ref, student_ref))
    ]
    for copy in copies:
        copy.start()
    for copy in copies:
        copy.wait()


def join_rows(teacher_rows, student_rows):
    count, depth = teacher_rows.shape
    return pl.pallas_call(
        join_kernel,
        in_specs=[pl.BlockSpec(memory_space=pltpu.HBM)] * 2,
        out_specs=pl.BlockSpec(memory_space=pltpu.VMEM),
        out_shape=jax.ShapeDtypeStruct((count, 2 * depth), teacher_rows.dtype),
        scratch_shapes=[pltpu.SemaphoreType.DMA((2,))],
        compiler_params=pltpu.CompilerParams(vmem_limit_bytes=2**20),
        cost_estimate=pl.CostEstimate(flops=0, bytes_accessed=8 * count * depth, transcendentals=0),
    )(stay(teacher_rows), stay(student_rows))


def gather_rows(teacher_rows, student_rows, n, fetch):
    join = lambda pair: jnp.concatenate(pair, axis=1)
    stack = lambda *parts: jnp.concatenate(parts, axis=0)
    far_teacher = swap(teacher_rows, 8, n)
    rows = join_rows(teacher_rows, student_rows)
    far_student = swap(student_rows, 8, n)
    near, side = swap(rows, 4, n), swap(rows, 2, n)
    *fetched, turned = fetch(rows)
    far = after(join((far_teacher, far_student)), *fetched, turned)
    far_near = swap(far, 4, n)
    other_head = swap(after(turned, far), 1, n)
    far_side = swap(far, 2, n)
    near_side = swap(side, 4, n)
    far_near_side = swap(far_near, 2, n)
    held = [stack(rows, side, near, near_side, far, far_side), stack(far_near, far_near_side)]
    return held + [swap(piece, 1, n) for piece in held], fetched, (turned, other_head)


def scatter_rows(near_keep, near_send, far_keep, far_send, rows_local, n, head_gradient_of, loss_of):
    low = jnp.bfloat16
    full = jnp.float32
    far_other = swap(far_send, 2, n)
    near_other = swap(near_send, 4, n)
    grad_head = head_gradient_of(far_send)
    far = (far_keep + far_other.astype(full)).astype(low)
    from_far = swap(far[:rows_local], 8, n)
    from_far_near = swap(far[rows_local:], 12, n)
    loss = loss_of(far_send)
    near = near_keep + near_other.astype(full)
    from_side = swap(near[rows_local:].astype(low), 2, n)
    total = lax.optimization_barrier(near[:rows_local] + from_far.astype(full) + from_far_near.astype(full))
    total = total + from_side.astype(full)
    return total, grad_head, loss


def per_device(n, teacher_hidden, student_hidden, teacher_head, student_head, labels, order):
    rows_local, depth = student_hidden.shape
    tuned = n == 16 and rows_local == 8
    me = lax.axis_index("dp").astype(jnp.int32).reshape(1)
    heads = (teacher_head, student_head)
    fetch = lambda *done: prepare(after(me, *done), order, labels, heads, rows_local, tuned)
    if tuned:
        hidden, fetched, turned = gather_rows(teacher_hidden, student_hidden, n, fetch)
    else:
        fetched = fetch(me)
        rows = jnp.concatenate([teacher_hidden, student_hidden], axis=1)
        hidden = [lax.all_gather(rows, "dp", axis=0, tiled=True)]
    *heads, pick, label = fetched
    *logit, stats = logits(me, pick, label, hidden, heads, n, rows_local, tuned)
    if tuned:
        stats, away = logit.pop(), swap(stats, 1, n)
    stats = lax.all_to_all(stats, "dp", 0, 0)
    head_gradient_of = lambda *done: head_gradient(
        after(me, *done), label, stats, logit, hidden, depth, rows_local, tuned
    )
    loss_of = lambda *done: row_loss(after(me, *done), stats, rows_local)
    if tuned:
        parts = gradient(me, label, stats, (*logit, away), turned, rows_local, tuned)
        grad_hidden, grad_head, loss = scatter_rows(*parts, rows_local, n, head_gradient_of, loss_of)
    else:
        (part,) = gradient(me, label, stats, logit, heads[1:], rows_local, tuned)
        grad_head, loss = head_gradient_of(part), loss_of(part)
        grad_hidden = lax.psum_scatter(part, "dp", scatter_dimension=0, tiled=True)
    return (loss[0, :rows_local], grad_hidden, grad_head)


def solution(mesh):
    in_specs = (
        P(("groups", "dp"), None),
        P(("groups", "dp"), None),
        P(None, "dp"),
        P(None, "dp"),
        P("groups"),
        P("groups"),
    )
    out_specs = (P(("groups", "dp")), P(("groups", "dp"), None), P("groups", "dp"))
    return jax.shard_map(
        functools.partial(per_device, mesh.shape["dp"]),
        mesh=mesh,
        in_specs=in_specs,
        out_specs=out_specs,
        check_vma=False,
    )
```

```python
import functools

import jax
import jax.numpy as jnp
from jax import lax
from jax.experimental import pallas as pl
from jax.experimental.pallas import tpu as pltpu
from jax.sharding import PartitionSpec as P

CE_WEIGHT = 0.5
VMEM_LIMIT = 28 * 2**20
STATS = 4


def held_rows(shape, dim, me, rows_local, tuned):
    held = lax.broadcasted_iota(jnp.int32, shape, dim)
    if not tuned:
        return held
    step = rows_local.bit_length() - 1
    block = lax.shift_right_logical(held, step)
    distance = (block & 7) * 2 + lax.shift_right_logical(block, 3)
    return (me ^ distance) * rows_local + (held & (rows_local - 1))


def to_column(is_row, row):
    return jnp.sum(jnp.where(is_row, row, 0.0), axis=1, keepdims=True)


def prepare_kernel(rows_local, tuned, me_ref, order_ref, labels_ref, *refs):
    teacher_ref, student_ref, teacher_out, student_out, pick_out, label_out, *turned_out = refs[: -4]
    ids, id_sems, teacher_sem, student_sems = refs[-4:]
    id_copies = [
        pltpu.make_async_copy(source, ids.at[j], id_sems.at[j]) for j, source in enumerate((order_ref, labels_ref))
    ]
    pieces = student_sems.shape[0]
    rows = student_ref.shape[0] // pieces
    parts = [pl.ds(k * rows, rows) for k in range(pieces)]
    copies = [
        pltpu.make_async_copy(student_ref.at[part], student_out.at[part], student_sems.at[k])
        for k, part in enumerate(parts)
    ]
    copies.append(pltpu.make_async_copy(teacher_ref, teacher_out, teacher_sem))
    for copy in id_copies + copies:
        copy.start()
    me = me_ref[0]
    count = order_ref.shape[1]
    vocab = teacher_ref.shape[1]
    lanes = lax.broadcasted_iota(jnp.int32, (count, count), 1)
    is_row = held_rows((count, count), 0, me, rows_local, tuned) == lanes
    have = held_rows((count, count), 1, me, rows_local, tuned).astype(jnp.float32)
    for copy in id_copies:
        copy.wait()
    wanted = to_column(is_row, ids[0].astype(jnp.float32))
    pick_out[...] = jnp.where(wanted == have, 1.0, 0.0).astype(jnp.bfloat16)
    label = to_column(is_row, ids[1].astype(jnp.float32)) - (me * vocab).astype(jnp.float32)
    label_out[...] = jnp.broadcast_to(label, label_out.shape)
    for k, copy in enumerate(copies):
        copy.wait()
        if k < pieces:
            for out in turned_out:
                out[:, k * rows : (k + 1) * rows] = student_out[k * rows : (k + 1) * rows].T


def stay(value):
    return pltpu.with_memory_space_constraint(value, pltpu.HBM)


def prepare(me, order, labels, heads, rows_local, tuned):
    count = order.shape[0]
    vmem = pl.BlockSpec(memory_space=pltpu.VMEM)
    hbm = pl.BlockSpec(memory_space=pltpu.HBM)
    shapes = [
        jax.ShapeDtypeStruct(heads[0].shape, heads[0].dtype),
        jax.ShapeDtypeStruct(heads[1].shape, heads[1].dtype),
        jax.ShapeDtypeStruct((count, count), jnp.bfloat16),
        jax.ShapeDtypeStruct((count, 128), jnp.float32),
    ] + [jax.ShapeDtypeStruct(heads[1].shape[::-1], heads[1].dtype)] * tuned
    return pl.pallas_call(
        functools.partial(prepare_kernel, rows_local, tuned),
        in_specs=[pl.BlockSpec(memory_space=pltpu.SMEM)] + [hbm] * 4,
        out_specs=(vmem,) * len(shapes),
        out_shape=tuple(shapes),
        scratch_shapes=[
            pltpu.VMEM((2, 1, count), jnp.int32),
            pltpu.SemaphoreType.DMA((2,)),
            pltpu.SemaphoreType.DMA,
            pltpu.SemaphoreType.DMA((8,)),
        ],
        compiler_params=pltpu.CompilerParams(vmem_limit_bytes=24 * 2**20),
        cost_estimate=pl.CostEstimate(flops=0, bytes_accessed=heads[0].size * 8, transcendentals=0),
    )(me, stay(order[None]), stay(labels[None]), *map(stay, heads))


def logits_kernel(rows_local, tuned, parts, me_ref, pick_ref, label_ref, *refs):
    pieces = refs[:parts]
    teacher_head, student_head, teacher_out, student_out, stats_out, *away_out = refs[parts:]
    depth, vocab = student_head.shape

    def product(first, head):
        rows = jnp.concatenate([piece[:, first : first + depth] for piece in pieces], axis=0)
        return jnp.dot(rows, head[...], preferred_element_type=jnp.float32)

    me = me_ref[0]
    raw = product(0, teacher_head)
    student = product(depth, student_head)
    count = student.shape[0]
    high = raw.astype(jnp.bfloat16)
    rest = raw - high.astype(jnp.float32)
    middle = rest.astype(jnp.bfloat16)
    low = (rest - middle.astype(jnp.float32)).astype(jnp.bfloat16)
    pick = pick_ref[...]
    teacher = sum(jnp.dot(pick, piece, preferred_element_type=jnp.float32) for piece in (high, middle, low))
    teacher_out[...] = teacher
    student_out[...] = student
    for out in away_out:
        out[0] = teacher[count // 2 :]
        out[1] = student[count // 2 :]
    is_label = label_ref[:, 0:1].astype(jnp.int32) == lax.broadcasted_iota(jnp.int32, (count, vocab), 1)
    teacher_max = jnp.max(teacher, axis=1, keepdims=True)
    student_max = jnp.max(student, axis=1, keepdims=True)
    teacher_exp = jnp.exp(teacher - teacher_max)
    teacher_total = jnp.sum(teacher_exp, axis=1, keepdims=True)
    student_total = jnp.sum(jnp.exp(student - student_max), axis=1, keepdims=True)
    values = (
        teacher_max + jnp.log(teacher_total),
        student_max + jnp.log(student_total),
        jnp.sum(teacher_exp * (teacher - student), axis=1, keepdims=True) / teacher_total,
        jnp.sum(jnp.where(is_label, student, 0.0), axis=1, keepdims=True),
    )
    lanes = lax.broadcasted_iota(jnp.int32, (count, count), 1)
    is_row = held_rows((count, count), 0, me, rows_local, tuned) == lanes
    block = [jnp.sum(jnp.where(is_row, value, 0.0), axis=0, keepdims=True) for value in values]
    stats_out[...] = jnp.broadcast_to(jnp.concatenate(block, axis=0)[None], stats_out.shape)


def logits(me, pick, label, hidden, heads, n, rows_local, tuned):
    count = pick.shape[0]
    depth, vocab = heads[0].shape
    vmem = pl.BlockSpec(memory_space=pltpu.VMEM)
    shapes = [(count, vocab), (count, vocab), (n, STATS, count)] + [(2, count // 2, vocab)] * tuned
    return pl.pallas_call(
        functools.partial(logits_kernel, rows_local, tuned, len(hidden)),
        in_specs=[pl.BlockSpec(memory_space=pltpu.SMEM)] + [vmem] * (4 + len(hidden)),
        out_specs=(vmem,) * len(shapes),
        out_shape=tuple(jax.ShapeDtypeStruct(shape, jnp.float32) for shape in shapes),
        compiler_params=pltpu.CompilerParams(vmem_limit_bytes=VMEM_LIMIT),
        cost_estimate=pl.CostEstimate(
            flops=4 * count * depth * vocab, bytes_accessed=4 * depth * (vocab + count), transcendentals=2 * count * vocab
        ),
    )(me, pick, label, *hidden, *heads)


def merged(stats_ref):
    devices, _, count = stats_ref.shape
    top = stats_ref[0, 0:2]
    for d in range(1, devices):
        top = jnp.maximum(top, stats_ref[d, 0:2])
    totals = jnp.zeros((2, count), jnp.float32)
    cross = jnp.zeros((1, count), jnp.float32)
    label_logit = jnp.zeros((1, count), jnp.float32)
    for d in range(devices):
        weight = jnp.exp(stats_ref[d, 0:2] - top)
        totals += weight
        cross += weight[0:1] * stats_ref[d, 2:3]
        label_logit += stats_ref[d, 3:4]
    return top + jnp.log(totals), cross / totals[0:1], label_logit


def logit_gradient(teacher, student, norms, is_row, label):
    is_label = label.astype(jnp.int32) == lax.broadcasted_iota(jnp.int32, student.shape, 1)
    return (
        (1.0 + CE_WEIGHT) * jnp.exp(student - to_column(is_row, norms[1:2]))
        - jnp.exp(teacher - to_column(is_row, norms[0:1]))
        - jnp.where(is_label, CE_WEIGHT, 0.0)
    ).astype(jnp.bfloat16)


def times_transposed(grad, head):
    return lax.dot_general(grad, head, (((1,), (1,)), ((), ())), preferred_element_type=jnp.float32)


def grad_kernel(
    rows_local, me_ref, label_ref, stats_ref, teacher_ref, student_ref, away_ref, turned_ref, other_ref, *outs
):
    near_keep, near_send, far_keep, far_send = outs
    me = me_ref[0]
    count, vocab = student_ref.shape
    own = count // 2
    norms = merged(stats_ref)[0]
    is_row = held_rows((own, count), 0, me, rows_local, True) == lax.broadcasted_iota(jnp.int32, (own, count), 1)
    label = label_ref[:own, 0:1]
    grad = logit_gradient(teacher_ref[:own], student_ref[:own], norms, is_row, label)
    shift = jnp.where((me & 1) == 0, -vocab, vocab).astype(jnp.float32)
    other = logit_gradient(away_ref[0], away_ref[1], norms, is_row, label + shift)
    depth = turned_ref.shape[1]
    step = min(512, depth)
    for k in range(0, depth, step):
        part = jnp.dot(grad, turned_ref[:, k : k + step], preferred_element_type=jnp.float32)
        part += jnp.dot(other, other_ref[:, k : k + step], preferred_element_type=jnp.float32)
        blocks = [part[b * rows_local : (b + 1) * rows_local] for b in range(8)]
        for out, first, second in ((near_keep, 0, 1), (near_send, 2, 3), (far_keep, 4, 6), (far_send, 5, 7)):
            out[:, k : k + step] = jnp.concatenate((blocks[first], blocks[second]), axis=0).astype(out.dtype)


def whole_grad_kernel(rows_local, me_ref, label_ref, stats_ref, teacher_ref, student_ref, head_ref, out_ref):
    count, vocab = student_ref.shape
    norms = merged(stats_ref)[0]
    is_row = held_rows((count, count), 0, me_ref[0], rows_local, False) == lax.broadcasted_iota(
        jnp.int32, (count, count), 1
    )
    grad = logit_gradient(teacher_ref[...], student_ref[...], norms, is_row, label_ref[:, 0:1])
    depth = head_ref.shape[0]
    step = min(512, depth)
    for k in range(0, depth, step):
        out_ref[:, k : k + step] = times_transposed(grad, head_ref[k : k + step])


def gradient(me, label, stats, logits, heads, rows_local, tuned):
    count, vocab = logits[0].shape
    depth = heads[0].shape[1 if tuned else 0]
    vmem = pl.BlockSpec(memory_space=pltpu.VMEM)
    if tuned:
        shapes = [jax.ShapeDtypeStruct((2 * rows_local, depth), kind) for kind in (jnp.float32, jnp.bfloat16)] * 2
    else:
        shapes = [jax.ShapeDtypeStruct((count, depth), jnp.float32)]
    return pl.pallas_call(
        functools.partial(grad_kernel if tuned else whole_grad_kernel, rows_local),
        in_specs=[pl.BlockSpec(memory_space=pltpu.SMEM)] + [vmem] * (2 + len(logits) + len(heads)),
        out_specs=(vmem,) * len(shapes),
        out_shape=tuple(shapes),
        compiler_params=pltpu.CompilerParams(vmem_limit_bytes=VMEM_LIMIT),
        cost_estimate=pl.CostEstimate(
            flops=2 * count * depth * vocab, bytes_accessed=2 * depth * (vocab + 2 * count), transcendentals=2 * count * vocab
        ),
    )(me, label, stats, *logits, *heads)


def head_kernel(rows_local, tuned, me_ref, label_ref, stats_ref, teacher_ref, student_ref, *refs):
    *pieces, out_ref, held, sems = refs
    me = me_ref[0]
    count = student_ref.shape[0]
    lanes = lax.broadcasted_iota(jnp.int32, (count, count), 1)
    is_row = held_rows((count, count), 0, me, rows_local, tuned) == lanes
    norms = merged(stats_ref)[0]
    grad = logit_gradient(teacher_ref[...], student_ref[...], norms, is_row, label_ref[:, 0:1])
    steps, step, _ = held.shape
    copies = []
    for k in range(steps):
        first = (steps + k) * step
        rows = jnp.concatenate([piece[:, first : first + step] for piece in pieces], axis=0)
        held[k] = lax.dot_general(rows, grad, (((0,), (0,)), ((), ())), preferred_element_type=jnp.float32).astype(
            jnp.bfloat16
        )
        copies.append(pltpu.make_async_copy(held.at[k], out_ref.at[pl.ds(k * step, step)], sems.at[k]))
        copies[-1].start()
    for copy in copies:
        copy.wait()


def head_gradient(me, label, stats, logits, hidden, depth, rows_local, tuned):
    count, vocab = logits[0].shape
    step = min(256, depth)
    vmem = pl.BlockSpec(memory_space=pltpu.VMEM)
    return pl.pallas_call(
        functools.partial(head_kernel, rows_local, tuned),
        in_specs=[pl.BlockSpec(memory_space=pltpu.SMEM)] + [vmem] * (4 + len(hidden)),
        out_specs=pl.BlockSpec(memory_space=pltpu.HBM),
        out_shape=jax.ShapeDtypeStruct((depth, vocab), jnp.bfloat16),
        scratch_shapes=[
            pltpu.VMEM((depth // step, step, vocab), jnp.bfloat16),
            pltpu.SemaphoreType.DMA((depth // step,)),
        ],
        compiler_params=pltpu.CompilerParams(vmem_limit_bytes=VMEM_LIMIT),
        cost_estimate=pl.CostEstimate(
            flops=2 * count * depth * vocab, bytes_accessed=2 * depth * (vocab + count), transcendentals=2 * count * vocab
        ),
    )(me, label, stats, *logits, *hidden)


def loss_kernel(rows_local, me_ref, stats_ref, loss_out):
    count = stats_ref.shape[2]
    norms, cross, label_logit = merged(stats_ref)
    loss = cross - norms[0:1] + norms[1:2] + CE_WEIGHT * (norms[1:2] - label_logit)
    lanes = lax.broadcasted_iota(jnp.int32, (count, count), 1)
    mine = lax.broadcasted_iota(jnp.int32, (count, count), 0) + me_ref[0] * rows_local == lanes
    by_lane = lax.broadcasted_iota(jnp.int32, (count, count), 0) == lanes
    loss_out[...] = jnp.sum(jnp.where(by_lane, to_column(mine, loss), 0.0), axis=0, keepdims=True)


def row_loss(me, stats, rows_local):
    vmem = pl.BlockSpec(memory_space=pltpu.VMEM)
    return pl.pallas_call(
        functools.partial(loss_kernel, rows_local),
        in_specs=[pl.BlockSpec(memory_space=pltpu.SMEM), vmem],
        out_specs=vmem,
        out_shape=jax.ShapeDtypeStruct((1, stats.shape[2]), jnp.float32),
        compiler_params=pltpu.CompilerParams(vmem_limit_bytes=VMEM_LIMIT),
        cost_estimate=pl.CostEstimate(flops=0, bytes_accessed=stats.size * 4, transcendentals=stats.size // 4),
    )(me, stats)


def swap(value, distance, n):
    return lax.ppermute(value, "dp", [(i, i ^ distance) for i in range(n)])


def after(value, *done):
    return lax.optimization_barrier((value, *done))[0]


def gather_rows(teacher_rows, student_rows, n, fetch):
    join = lambda pair: jnp.concatenate(pair, axis=1)
    stack = lambda *parts: jnp.concatenate(parts, axis=0)
    far_teacher = swap(teacher_rows, 8, n)
    rows = join((teacher_rows, student_rows))
    far_student = swap(student_rows, 8, n)
    near, side = swap(rows, 4, n), swap(rows, 2, n)
    *fetched, turned = fetch(rows)
    far = after(join((far_teacher, far_student)), *fetched, turned)
    far_near = swap(far, 4, n)
    other_head = swap(after(turned, far), 1, n)
    far_side = swap(far, 2, n)
    near_side = swap(side, 4, n)
    far_near_side = swap(far_near, 2, n)
    held = [stack(rows, side, near, near_side, far, far_side), stack(far_near, far_near_side)]
    return held + [swap(piece, 1, n) for piece in held], fetched, (turned, other_head)


def scatter_rows(near_keep, near_send, far_keep, far_send, rows_local, n, head_gradient_of, loss_of):
    low = jnp.bfloat16
    full = jnp.float32
    far_other = swap(far_send, 2, n)
    near_other = swap(near_send, 4, n)
    grad_head = head_gradient_of(far_send)
    far = (far_keep + far_other.astype(full)).astype(low)
    from_far = swap(far[:rows_local], 8, n)
    from_far_near = swap(far[rows_local:], 12, n)
    loss = loss_of(far_send)
    near = near_keep + near_other.astype(full)
    from_side = swap(near[rows_local:].astype(low), 2, n)
    total = lax.optimization_barrier(near[:rows_local] + from_far.astype(full) + from_far_near.astype(full))
    total = total + from_side.astype(full)
    return total, grad_head, loss


def per_device(n, teacher_hidden, student_hidden, teacher_head, student_head, labels, order):
    rows_local, depth = student_hidden.shape
    tuned = n == 16 and rows_local == 8
    me = lax.axis_index("dp").astype(jnp.int32).reshape(1)
    heads = (teacher_head, student_head)
    fetch = lambda *done: prepare(after(me, *done), order, labels, heads, rows_local, tuned)
    if tuned:
        hidden, fetched, turned = gather_rows(teacher_hidden, student_hidden, n, fetch)
    else:
        fetched = fetch(me)
        rows = jnp.concatenate([teacher_hidden, student_hidden], axis=1)
        hidden = [lax.all_gather(rows, "dp", axis=0, tiled=True)]
    *heads, pick, label = fetched
    *logit, stats = logits(me, pick, label, hidden, heads, n, rows_local, tuned)
    if tuned:
        stats, away = logit.pop(), swap(stats, 1, n)
    stats = lax.all_to_all(stats, "dp", 0, 0)
    head_gradient_of = lambda *done: head_gradient(
        after(me, *done), label, stats, logit, hidden, depth, rows_local, tuned
    )
    loss_of = lambda *done: row_loss(after(me, *done), stats, rows_local)
    if tuned:
        parts = gradient(me, label, stats, (*logit, away), turned, rows_local, tuned)
        grad_hidden, grad_head, loss = scatter_rows(*parts, rows_local, n, head_gradient_of, loss_of)
    else:
        (part,) = gradient(me, label, stats, logit, heads[1:], rows_local, tuned)
        grad_head, loss = head_gradient_of(part), loss_of(part)
        grad_hidden = lax.psum_scatter(part, "dp", scatter_dimension=0, tiled=True)
    return (loss[0, :rows_local], grad_hidden, grad_head)


def solution(mesh):
    in_specs = (
        P(("groups", "dp"), None),
        P(("groups", "dp"), None),
        P(None, "dp"),
        P(None, "dp"),
        P("groups"),
        P("groups"),
    )
    out_specs = (P(("groups", "dp")), P(("groups", "dp"), None), P("groups", "dp"))
    return jax.shard_map(
        functools.partial(per_device, mesh.shape["dp"]),
        mesh=mesh,
        in_specs=in_specs,
        out_specs=out_specs,
        check_vma=False,
    )
```

```python
import functools

import jax
import jax.numpy as jnp
from jax import lax
from jax.experimental import pallas as pl
from jax.experimental.pallas import tpu as pltpu
from jax.sharding import PartitionSpec as P

CE_WEIGHT = 0.5
VMEM_LIMIT = 28 * 2**20
STATS = 4


def held_rows(shape, dim, me, rows_local, tuned):
    held = lax.broadcasted_iota(jnp.int32, shape, dim)
    if not tuned:
        return held
    step = rows_local.bit_length() - 1
    block = lax.shift_right_logical(held, step)
    distance = (block & 7) * 2 + lax.shift_right_logical(block, 3)
    return (me ^ distance) * rows_local + (held & (rows_local - 1))


def to_column(is_row, row):
    return jnp.sum(jnp.where(is_row, row, 0.0), axis=1, keepdims=True)


def prepare_kernel(rows_local, tuned, me_ref, order_ref, labels_ref, *refs):
    teacher_ref, student_ref, teacher_out, student_out, pick_out, label_out, *turned_out = refs[: -4]
    ids, id_sems, teacher_sem, student_sems = refs[-4:]
    id_copies = [
        pltpu.make_async_copy(source, ids.at[j], id_sems.at[j]) for j, source in enumerate((order_ref, labels_ref))
    ]
    pieces = student_sems.shape[0]
    rows = student_ref.shape[0] // pieces
    parts = [pl.ds(k * rows, rows) for k in range(pieces)]
    copies = [
        pltpu.make_async_copy(student_ref.at[part], student_out.at[part], student_sems.at[k])
        for k, part in enumerate(parts)
    ]
    copies.append(pltpu.make_async_copy(teacher_ref, teacher_out, teacher_sem))
    for copy in id_copies + copies:
        copy.start()
    me = me_ref[0]
    count = order_ref.shape[1]
    vocab = teacher_ref.shape[1]
    lanes = lax.broadcasted_iota(jnp.int32, (count, count), 1)
    is_row = held_rows((count, count), 0, me, rows_local, tuned) == lanes
    have = held_rows((count, count), 1, me, rows_local, tuned).astype(jnp.float32)
    for copy in id_copies:
        copy.wait()
    wanted = to_column(is_row, ids[0].astype(jnp.float32))
    pick_out[...] = jnp.where(wanted == have, 1.0, 0.0).astype(jnp.bfloat16)
    label = to_column(is_row, ids[1].astype(jnp.float32)) - (me * vocab).astype(jnp.float32)
    label_out[...] = jnp.broadcast_to(label, label_out.shape)
    for k, copy in enumerate(copies):
        copy.wait()
        if k < pieces:
            for out in turned_out:
                out[:, k * rows : (k + 1) * rows] = student_out[k * rows : (k + 1) * rows].T


def stay(value):
    return pltpu.with_memory_space_constraint(value, pltpu.HBM)


def prepare(me, order, labels, heads, rows_local, tuned):
    count = order.shape[0]
    vmem = pl.BlockSpec(memory_space=pltpu.VMEM)
    hbm = pl.BlockSpec(memory_space=pltpu.HBM)
    shapes = [
        jax.ShapeDtypeStruct(heads[0].shape, heads[0].dtype),
        jax.ShapeDtypeStruct(heads[1].shape, heads[1].dtype),
        jax.ShapeDtypeStruct((count, count), jnp.bfloat16),
        jax.ShapeDtypeStruct((count, 128), jnp.float32),
    ] + [jax.ShapeDtypeStruct(heads[1].shape[::-1], heads[1].dtype)] * tuned
    return pl.pallas_call(
        functools.partial(prepare_kernel, rows_local, tuned),
        in_specs=[pl.BlockSpec(memory_space=pltpu.SMEM)] + [hbm] * 4,
        out_specs=(vmem,) * len(shapes),
        out_shape=tuple(shapes),
        scratch_shapes=[
            pltpu.VMEM((2, 1, count), jnp.int32),
            pltpu.SemaphoreType.DMA((2,)),
            pltpu.SemaphoreType.DMA,
            pltpu.SemaphoreType.DMA((8,)),
        ],
        compiler_params=pltpu.CompilerParams(vmem_limit_bytes=24 * 2**20),
        cost_estimate=pl.CostEstimate(flops=0, bytes_accessed=heads[0].size * 8, transcendentals=0),
    )(me, stay(order[None]), stay(labels[None]), *map(stay, heads))


def logits_kernel(rows_local, tuned, parts, me_ref, pick_ref, label_ref, *refs):
    pieces = refs[:parts]
    teacher_head, student_head, teacher_out, student_out, stats_out, *away_out = refs[parts:]
    depth, vocab = student_head.shape

    def product(first, head):
        rows = jnp.concatenate([piece[:, first : first + depth] for piece in pieces], axis=0)
        return jnp.dot(rows, head[...], preferred_element_type=jnp.float32)

    me = me_ref[0]
    raw = product(0, teacher_head)
    student = product(depth, student_head)
    count = student.shape[0]
    high = raw.astype(jnp.bfloat16)
    rest = raw - high.astype(jnp.float32)
    middle = rest.astype(jnp.bfloat16)
    low = (rest - middle.astype(jnp.float32)).astype(jnp.bfloat16)
    pick = pick_ref[...]
    teacher = jnp.dot(
        jnp.concatenate((pick, pick, pick), axis=1),
        jnp.concatenate((high, middle, low), axis=0),
        preferred_element_type=jnp.float32,
    )
    teacher_out[...] = teacher
    student_out[...] = student
    for out in away_out:
        out[0] = teacher[count // 2 :]
        out[1] = student[count // 2 :]
    is_label = label_ref[:, 0:1].astype(jnp.int32) == lax.broadcasted_iota(jnp.int32, (count, vocab), 1)
    teacher_max = jnp.max(teacher, axis=1, keepdims=True)
    student_max = jnp.max(student, axis=1, keepdims=True)
    teacher_exp = jnp.exp(teacher - teacher_max)
    teacher_total = jnp.sum(teacher_exp, axis=1, keepdims=True)
    student_total = jnp.sum(jnp.exp(student - student_max), axis=1, keepdims=True)
    values = (
        teacher_max + jnp.log(teacher_total),
        student_max + jnp.log(student_total),
        jnp.sum(teacher_exp * (teacher - student), axis=1, keepdims=True) / teacher_total,
        jnp.sum(jnp.where(is_label, student, 0.0), axis=1, keepdims=True),
    )
    lanes = lax.broadcasted_iota(jnp.int32, (count, count), 1)
    is_row = held_rows((count, count), 0, me, rows_local, tuned) == lanes
    block = [jnp.sum(jnp.where(is_row, value, 0.0), axis=0, keepdims=True) for value in values]
    stats_out[...] = jnp.broadcast_to(jnp.concatenate(block, axis=0)[None], stats_out.shape)


def logits(me, pick, label, hidden, heads, n, rows_local, tuned):
    count = pick.shape[0]
    depth, vocab = heads[0].shape
    vmem = pl.BlockSpec(memory_space=pltpu.VMEM)
    shapes = [(count, vocab), (count, vocab), (n, STATS, count)] + [(2, count // 2, vocab)] * tuned
    return pl.pallas_call(
        functools.partial(logits_kernel, rows_local, tuned, len(hidden)),
        in_specs=[pl.BlockSpec(memory_space=pltpu.SMEM)] + [vmem] * (4 + len(hidden)),
        out_specs=(vmem,) * len(shapes),
        out_shape=tuple(jax.ShapeDtypeStruct(shape, jnp.float32) for shape in shapes),
        compiler_params=pltpu.CompilerParams(vmem_limit_bytes=VMEM_LIMIT),
        cost_estimate=pl.CostEstimate(
            flops=4 * count * depth * vocab, bytes_accessed=4 * depth * (vocab + count), transcendentals=2 * count * vocab
        ),
    )(me, pick, label, *hidden, *heads)


def merged(stats_ref):
    devices, _, count = stats_ref.shape
    top = stats_ref[0, 0:2]
    for d in range(1, devices):
        top = jnp.maximum(top, stats_ref[d, 0:2])
    totals = jnp.zeros((2, count), jnp.float32)
    cross = jnp.zeros((1, count), jnp.float32)
    label_logit = jnp.zeros((1, count), jnp.float32)
    for d in range(devices):
        weight = jnp.exp(stats_ref[d, 0:2] - top)
        totals += weight
        cross += weight[0:1] * stats_ref[d, 2:3]
        label_logit += stats_ref[d, 3:4]
    return top + jnp.log(totals), cross / totals[0:1], label_logit


def logit_gradient(teacher, student, norms, is_row, label):
    is_label = label.astype(jnp.int32) == lax.broadcasted_iota(jnp.int32, student.shape, 1)
    return (
        (1.0 + CE_WEIGHT) * jnp.exp(student - to_column(is_row, norms[1:2]))
        - jnp.exp(teacher - to_column(is_row, norms[0:1]))
        - jnp.where(is_label, CE_WEIGHT, 0.0)
    ).astype(jnp.bfloat16)


def times_transposed(grad, head):
    return lax.dot_general(grad, head, (((1,), (1,)), ((), ())), preferred_element_type=jnp.float32)


def grad_kernel(
    rows_local, me_ref, label_ref, stats_ref, teacher_ref, student_ref, away_ref, turned_ref, other_ref, *outs
):
    near_keep, near_send, far_keep, far_send = outs
    me = me_ref[0]
    count, vocab = student_ref.shape
    own = count // 2
    norms = merged(stats_ref)[0]
    is_row = held_rows((own, count), 0, me, rows_local, True) == lax.broadcasted_iota(jnp.int32, (own, count), 1)
    label = label_ref[:own, 0:1]
    grad = logit_gradient(teacher_ref[:own], student_ref[:own], norms, is_row, label)
    shift = jnp.where((me & 1) == 0, -vocab, vocab).astype(jnp.float32)
    other = logit_gradient(away_ref[0], away_ref[1], norms, is_row, label + shift)
    grads = jnp.concatenate((grad, other), axis=1)
    depth = turned_ref.shape[1]
    step = min(512, depth)
    for k in range(0, depth, step):
        heads = jnp.concatenate((turned_ref[:, k : k + step], other_ref[:, k : k + step]), axis=0)
        part = jnp.dot(grads, heads, preferred_element_type=jnp.float32)
        blocks = [part[b * rows_local : (b + 1) * rows_local] for b in range(8)]
        for out, first, second in ((near_keep, 0, 1), (near_send, 2, 3), (far_keep, 4, 6), (far_send, 5, 7)):
            out[:, k : k + step] = jnp.concatenate((blocks[first], blocks[second]), axis=0).astype(out.dtype)


def whole_grad_kernel(rows_local, me_ref, label_ref, stats_ref, teacher_ref, student_ref, head_ref, out_ref):
    count, vocab = student_ref.shape
    norms = merged(stats_ref)[0]
    is_row = held_rows((count, count), 0, me_ref[0], rows_local, False) == lax.broadcasted_iota(
        jnp.int32, (count, count), 1
    )
    grad = logit_gradient(teacher_ref[...], student_ref[...], norms, is_row, label_ref[:, 0:1])
    depth = head_ref.shape[0]
    step = min(512, depth)
    for k in range(0, depth, step):
        out_ref[:, k : k + step] = times_transposed(grad, head_ref[k : k + step])


def gradient(me, label, stats, logits, heads, rows_local, tuned):
    count, vocab = logits[0].shape
    depth = heads[0].shape[1 if tuned else 0]
    vmem = pl.BlockSpec(memory_space=pltpu.VMEM)
    if tuned:
        shapes = [jax.ShapeDtypeStruct((2 * rows_local, depth), kind) for kind in (jnp.float32, jnp.bfloat16)] * 2
    else:
        shapes = [jax.ShapeDtypeStruct((count, depth), jnp.float32)]
    return pl.pallas_call(
        functools.partial(grad_kernel if tuned else whole_grad_kernel, rows_local),
        in_specs=[pl.BlockSpec(memory_space=pltpu.SMEM)] + [vmem] * (2 + len(logits) + len(heads)),
        out_specs=(vmem,) * len(shapes),
        out_shape=tuple(shapes),
        compiler_params=pltpu.CompilerParams(vmem_limit_bytes=VMEM_LIMIT),
        cost_estimate=pl.CostEstimate(
            flops=2 * count * depth * vocab, bytes_accessed=2 * depth * (vocab + 2 * count), transcendentals=2 * count * vocab
        ),
    )(me, label, stats, *logits, *heads)


def head_kernel(rows_local, tuned, me_ref, label_ref, stats_ref, teacher_ref, student_ref, *refs):
    *pieces, out_ref, held, sems = refs
    me = me_ref[0]
    count = student_ref.shape[0]
    lanes = lax.broadcasted_iota(jnp.int32, (count, count), 1)
    is_row = held_rows((count, count), 0, me, rows_local, tuned) == lanes
    norms = merged(stats_ref)[0]
    grad = logit_gradient(teacher_ref[...], student_ref[...], norms, is_row, label_ref[:, 0:1])
    steps, step, _ = held.shape
    copies = []
    for k in range(steps):
        first = (steps + k) * step
        rows = jnp.concatenate([piece[:, first : first + step] for piece in pieces], axis=0)
        held[k] = lax.dot_general(rows, grad, (((0,), (0,)), ((), ())), preferred_element_type=jnp.float32).astype(
            jnp.bfloat16
        )
        copies.append(pltpu.make_async_copy(held.at[k], out_ref.at[pl.ds(k * step, step)], sems.at[k]))
        copies[-1].start()
    for copy in copies:
        copy.wait()


def head_gradient(me, label, stats, logits, hidden, depth, rows_local, tuned):
    count, vocab = logits[0].shape
    step = min(256, depth)
    vmem = pl.BlockSpec(memory_space=pltpu.VMEM)
    return pl.pallas_call(
        functools.partial(head_kernel, rows_local, tuned),
        in_specs=[pl.BlockSpec(memory_space=pltpu.SMEM)] + [vmem] * (4 + len(hidden)),
        out_specs=pl.BlockSpec(memory_space=pltpu.HBM),
        out_shape=jax.ShapeDtypeStruct((depth, vocab), jnp.bfloat16),
        scratch_shapes=[
            pltpu.VMEM((depth // step, step, vocab), jnp.bfloat16),
            pltpu.SemaphoreType.DMA((depth // step,)),
        ],
        compiler_params=pltpu.CompilerParams(vmem_limit_bytes=VMEM_LIMIT),
        cost_estimate=pl.CostEstimate(
            flops=2 * count * depth * vocab, bytes_accessed=2 * depth * (vocab + count), transcendentals=2 * count * vocab
        ),
    )(me, label, stats, *logits, *hidden)


def loss_kernel(rows_local, me_ref, stats_ref, loss_out):
    count = stats_ref.shape[2]
    norms, cross, label_logit = merged(stats_ref)
    loss = cross - norms[0:1] + norms[1:2] + CE_WEIGHT * (norms[1:2] - label_logit)
    lanes = lax.broadcasted_iota(jnp.int32, (count, count), 1)
    mine = lax.broadcasted_iota(jnp.int32, (count, count), 0) + me_ref[0] * rows_local == lanes
    by_lane = lax.broadcasted_iota(jnp.int32, (count, count), 0) == lanes
    loss_out[...] = jnp.sum(jnp.where(by_lane, to_column(mine, loss), 0.0), axis=0, keepdims=True)


def row_loss(me, stats, rows_local):
    vmem = pl.BlockSpec(memory_space=pltpu.VMEM)
    return pl.pallas_call(
        functools.partial(loss_kernel, rows_local),
        in_specs=[pl.BlockSpec(memory_space=pltpu.SMEM), vmem],
        out_specs=vmem,
        out_shape=jax.ShapeDtypeStruct((1, stats.shape[2]), jnp.float32),
        compiler_params=pltpu.CompilerParams(vmem_limit_bytes=VMEM_LIMIT),
        cost_estimate=pl.CostEstimate(flops=0, bytes_accessed=stats.size * 4, transcendentals=stats.size // 4),
    )(me, stats)


def swap(value, distance, n):
    return lax.ppermute(value, "dp", [(i, i ^ distance) for i in range(n)])


def after(value, *done):
    return lax.optimization_barrier((value, *done))[0]


def join_kernel(teacher_ref, student_ref, out_ref, sems):
    depth = teacher_ref.shape[1]
    copies = [
        pltpu.make_async_copy(ref, out_ref.at[:, pl.ds(j * depth, depth)], sems.at[j])
        for j, ref in enumerate((teacher_ref, student_ref))
    ]
    for copy in copies:
        copy.start()
    for copy in copies:
        copy.wait()


def join_rows(teacher_rows, student_rows):
    count, depth = teacher_rows.shape
    return pl.pallas_call(
        join_kernel,
        in_specs=[pl.BlockSpec(memory_space=pltpu.HBM)] * 2,
        out_specs=pl.BlockSpec(memory_space=pltpu.VMEM),
        out_shape=jax.ShapeDtypeStruct((count, 2 * depth), teacher_rows.dtype),
        scratch_shapes=[pltpu.SemaphoreType.DMA((2,))],
        compiler_params=pltpu.CompilerParams(vmem_limit_bytes=2**20),
        cost_estimate=pl.CostEstimate(flops=0, bytes_accessed=8 * count * depth, transcendentals=0),
    )(stay(teacher_rows), stay(student_rows))


def gather_rows(teacher_rows, student_rows, n, fetch):
    join = lambda pair: jnp.concatenate(pair, axis=1)
    stack = lambda *parts: jnp.concatenate(parts, axis=0)
    far_teacher = swap(teacher_rows, 8, n)
    rows = join_rows(teacher_rows, student_rows)
    far_student = swap(student_rows, 8, n)
    near, side = swap(rows, 4, n), swap(rows, 2, n)
    *fetched, turned = fetch(rows)
    far = after(join((far_teacher, far_student)), *fetched, turned)
    far_near = swap(far, 4, n)
    other_head = swap(after(turned, far), 1, n)
    far_side = swap(far, 2, n)
    near_side = swap(side, 4, n)
    far_near_side = swap(far_near, 2, n)
    held = [stack(rows, side, near, near_side, far, far_side), stack(far_near, far_near_side)]
    return held + [swap(piece, 1, n) for piece in held], fetched, (turned, other_head)


def scatter_rows(near_keep, near_send, far_keep, far_send, rows_local, n, head_gradient_of, loss_of):
    low = jnp.bfloat16
    full = jnp.float32
    far_other = swap(far_send, 2, n)
    near_other = swap(near_send, 4, n)
    grad_head = head_gradient_of(far_send)
    far = (far_keep + far_other.astype(full)).astype(low)
    from_far = swap(far[:rows_local], 8, n)
    from_far_near = swap(far[rows_local:], 12, n)
    loss = loss_of(far_send)
    near = near_keep + near_other.astype(full)
    from_side = swap(near[rows_local:].astype(low), 2, n)
    total = lax.optimization_barrier(near[:rows_local] + from_far.astype(full) + from_far_near.astype(full))
    total = total + from_side.astype(full)
    return total, grad_head, loss


def per_device(n, teacher_hidden, student_hidden, teacher_head, student_head, labels, order):
    rows_local, depth = student_hidden.shape
    tuned = n == 16 and rows_local == 8
    me = lax.axis_index("dp").astype(jnp.int32).reshape(1)
    heads = (teacher_head, student_head)
    fetch = lambda *done: prepare(after(me, *done), order, labels, heads, rows_local, tuned)
    if tuned:
        hidden, fetched, turned = gather_rows(teacher_hidden, student_hidden, n, fetch)
    else:
        fetched = fetch(me)
        rows = jnp.concatenate([teacher_hidden, student_hidden], axis=1)
        hidden = [lax.all_gather(rows, "dp", axis=0, tiled=True)]
    *heads, pick, label = fetched
    *logit, stats = logits(me, pick, label, hidden, heads, n, rows_local, tuned)
    if tuned:
        stats, away = logit.pop(), swap(stats, 1, n)
    stats = lax.all_to_all(stats, "dp", 0, 0)
    head_gradient_of = lambda *done: head_gradient(
        after(me, *done), label, stats, logit, hidden, depth, rows_local, tuned
    )
    loss_of = lambda *done: row_loss(after(me, *done), stats, rows_local)
    if tuned:
        parts = gradient(me, label, stats, (*logit, away), turned, rows_local, tuned)
        grad_hidden, grad_head, loss = scatter_rows(*parts, rows_local, n, head_gradient_of, loss_of)
    else:
        (part,) = gradient(me, label, stats, logit, heads[1:], rows_local, tuned)
        grad_head, loss = head_gradient_of(part), loss_of(part)
        grad_hidden = lax.psum_scatter(part, "dp", scatter_dimension=0, tiled=True)
    return (loss[0, :rows_local], grad_hidden, grad_head)


def solution(mesh):
    in_specs = (
        P(("groups", "dp"), None),
        P(("groups", "dp"), None),
        P(None, "dp"),
        P(None, "dp"),
        P("groups"),
        P("groups"),
    )
    out_specs = (P(("groups", "dp")), P(("groups", "dp"), None), P("groups", "dp"))
    return jax.shard_map(
        functools.partial(per_device, mesh.shape["dp"]),
        mesh=mesh,
        in_specs=in_specs,
        out_specs=out_specs,
        check_vma=False,
    )
```

```python
import functools

import jax
import jax.numpy as jnp
from jax import lax
from jax.experimental import pallas as pl
from jax.experimental.pallas import tpu as pltpu
from jax.sharding import PartitionSpec as P

CE_WEIGHT = 0.5
VMEM_LIMIT = 28 * 2**20
STATS = 4


def held_rows(shape, dim, me, rows_local, tuned):
    held = lax.broadcasted_iota(jnp.int32, shape, dim)
    if not tuned:
        return held
    step = rows_local.bit_length() - 1
    block = lax.shift_right_logical(held, step)
    distance = (block & 7) * 2 + lax.shift_right_logical(block, 3)
    return (me ^ distance) * rows_local + (held & (rows_local - 1))


def to_column(is_row, row):
    return jnp.sum(jnp.where(is_row, row, 0.0), axis=1, keepdims=True)


def prepare_kernel(rows_local, tuned, me_ref, order_ref, labels_ref, *refs):
    teacher_ref, student_ref, teacher_out, student_out, pick_out, label_out, *turned_out = refs[: -4]
    ids, id_sems, teacher_sem, student_sems = refs[-4:]
    id_copies = [
        pltpu.make_async_copy(source, ids.at[j], id_sems.at[j]) for j, source in enumerate((order_ref, labels_ref))
    ]
    pieces = student_sems.shape[0]
    rows = student_ref.shape[0] // pieces
    parts = [pl.ds(k * rows, rows) for k in range(pieces)]
    copies = [
        pltpu.make_async_copy(student_ref.at[part], student_out.at[part], student_sems.at[k])
        for k, part in enumerate(parts)
    ]
    copies.append(pltpu.make_async_copy(teacher_ref, teacher_out, teacher_sem))
    for copy in id_copies + copies:
        copy.start()
    me = me_ref[0]
    count = order_ref.shape[1]
    vocab = teacher_ref.shape[1]
    lanes = lax.broadcasted_iota(jnp.int32, (count, count), 1)
    is_row = held_rows((count, count), 0, me, rows_local, tuned) == lanes
    have = held_rows((count, count), 1, me, rows_local, tuned).astype(jnp.float32)
    for copy in id_copies:
        copy.wait()
    wanted = to_column(is_row, ids[0].astype(jnp.float32))
    pick_out[...] = jnp.where(wanted == have, 1.0, 0.0).astype(jnp.bfloat16)
    label = to_column(is_row, ids[1].astype(jnp.float32)) - (me * vocab).astype(jnp.float32)
    label_out[...] = jnp.broadcast_to(label, label_out.shape)
    for k, copy in enumerate(copies):
        copy.wait()
        if k < pieces:
            for out in turned_out:
                out[:, k * rows : (k + 1) * rows] = student_out[k * rows : (k + 1) * rows].T


def stay(value):
    return pltpu.with_memory_space_constraint(value, pltpu.HBM)


def prepare(me, order, labels, heads, rows_local, tuned):
    count = order.shape[0]
    vmem = pl.BlockSpec(memory_space=pltpu.VMEM)
    hbm = pl.BlockSpec(memory_space=pltpu.HBM)
    shapes = [
        jax.ShapeDtypeStruct(heads[0].shape, heads[0].dtype),
        jax.ShapeDtypeStruct(heads[1].shape, heads[1].dtype),
        jax.ShapeDtypeStruct((count, count), jnp.bfloat16),
        jax.ShapeDtypeStruct((count, 128), jnp.float32),
    ] + [jax.ShapeDtypeStruct(heads[1].shape[::-1], heads[1].dtype)] * tuned
    return pl.pallas_call(
        functools.partial(prepare_kernel, rows_local, tuned),
        in_specs=[pl.BlockSpec(memory_space=pltpu.SMEM)] + [hbm] * 4,
        out_specs=(vmem,) * len(shapes),
        out_shape=tuple(shapes),
        scratch_shapes=[
            pltpu.VMEM((2, 1, count), jnp.int32),
            pltpu.SemaphoreType.DMA((2,)),
            pltpu.SemaphoreType.DMA,
            pltpu.SemaphoreType.DMA((8,)),
        ],
        compiler_params=pltpu.CompilerParams(vmem_limit_bytes=24 * 2**20),
        cost_estimate=pl.CostEstimate(flops=0, bytes_accessed=heads[0].size * 8, transcendentals=0),
    )(me, stay(order[None]), stay(labels[None]), *map(stay, heads))


def logits_kernel(rows_local, tuned, parts, me_ref, pick_ref, label_ref, *refs):
    pieces = refs[:parts]
    teacher_head, student_head, teacher_out, student_out, stats_out, *away_out = refs[parts:]
    depth, vocab = student_head.shape

    def product(first, head):
        rows = jnp.concatenate([piece[:, first : first + depth] for piece in pieces], axis=0)
        return jnp.dot(rows, head[...], preferred_element_type=jnp.float32)

    me = me_ref[0]
    raw = product(0, teacher_head)
    student = product(depth, student_head)
    count = student.shape[0]
    high = raw.astype(jnp.bfloat16)
    rest = raw - high.astype(jnp.float32)
    middle = rest.astype(jnp.bfloat16)
    low = (rest - middle.astype(jnp.float32)).astype(jnp.bfloat16)
    pick = pick_ref[...]
    teacher = jnp.dot(
        jnp.concatenate((pick, pick, pick), axis=1),
        jnp.concatenate((high, middle, low), axis=0),
        preferred_element_type=jnp.float32,
    )
    teacher_out[...] = teacher
    student_out[...] = student
    for out in away_out:
        out[0] = teacher[count // 2 :]
        out[1] = student[count // 2 :]
    is_label = label_ref[:, 0:1].astype(jnp.int32) == lax.broadcasted_iota(jnp.int32, (count, vocab), 1)
    teacher_max = jnp.max(teacher, axis=1, keepdims=True)
    student_max = jnp.max(student, axis=1, keepdims=True)
    teacher_exp = jnp.exp(teacher - teacher_max)
    teacher_total = jnp.sum(teacher_exp, axis=1, keepdims=True)
    student_total = jnp.sum(jnp.exp(student - student_max), axis=1, keepdims=True)
    values = (
        teacher_max + jnp.log(teacher_total),
        student_max + jnp.log(student_total),
        jnp.sum(teacher_exp * (teacher - student), axis=1, keepdims=True) / teacher_total,
        jnp.sum(jnp.where(is_label, student, 0.0), axis=1, keepdims=True),
    )
    lanes = lax.broadcasted_iota(jnp.int32, (count, count), 1)
    is_row = held_rows((count, count), 0, me, rows_local, tuned) == lanes
    block = [jnp.sum(jnp.where(is_row, value, 0.0), axis=0, keepdims=True) for value in values]
    stats_out[...] = jnp.broadcast_to(jnp.concatenate(block, axis=0)[None], stats_out.shape)


def logits(me, pick, label, hidden, heads, n, rows_local, tuned):
    count = pick.shape[0]
    depth, vocab = heads[0].shape
    vmem = pl.BlockSpec(memory_space=pltpu.VMEM)
    shapes = [(count, vocab), (count, vocab), (n, STATS, count)] + [(2, count // 2, vocab)] * tuned
    return pl.pallas_call(
        functools.partial(logits_kernel, rows_local, tuned, len(hidden)),
        in_specs=[pl.BlockSpec(memory_space=pltpu.SMEM)] + [vmem] * (4 + len(hidden)),
        out_specs=(vmem,) * len(shapes),
        out_shape=tuple(jax.ShapeDtypeStruct(shape, jnp.float32) for shape in shapes),
        compiler_params=pltpu.CompilerParams(vmem_limit_bytes=VMEM_LIMIT),
        cost_estimate=pl.CostEstimate(
            flops=4 * count * depth * vocab, bytes_accessed=4 * depth * (vocab + count), transcendentals=2 * count * vocab
        ),
    )(me, pick, label, *hidden, *heads)


def merged(stats_ref):
    devices, _, count = stats_ref.shape
    top = stats_ref[0, 0:2]
    for d in range(1, devices):
        top = jnp.maximum(top, stats_ref[d, 0:2])
    totals = jnp.zeros((2, count), jnp.float32)
    cross = jnp.zeros((1, count), jnp.float32)
    label_logit = jnp.zeros((1, count), jnp.float32)
    for d in range(devices):
        weight = jnp.exp(stats_ref[d, 0:2] - top)
        totals += weight
        cross += weight[0:1] * stats_ref[d, 2:3]
        label_logit += stats_ref[d, 3:4]
    return top + jnp.log(totals), cross / totals[0:1], label_logit


def logit_gradient(teacher, student, norms, is_row, label):
    is_label = label.astype(jnp.int32) == lax.broadcasted_iota(jnp.int32, student.shape, 1)
    return (
        (1.0 + CE_WEIGHT) * jnp.exp(student - to_column(is_row, norms[1:2]))
        - jnp.exp(teacher - to_column(is_row, norms[0:1]))
        - jnp.where(is_label, CE_WEIGHT, 0.0)
    ).astype(jnp.bfloat16)


def times_transposed(grad, head):
    return lax.dot_general(grad, head, (((1,), (1,)), ((), ())), preferred_element_type=jnp.float32)


def grad_kernel(
    rows_local, me_ref, label_ref, stats_ref, teacher_ref, student_ref, away_ref, turned_ref, other_ref, *outs
):
    near_keep, near_send, far_keep, far_send, norms_out = outs
    me = me_ref[0]
    count, vocab = student_ref.shape
    own = count // 2
    norms = merged(stats_ref)[0]
    norms_out[...] = norms
    is_row = held_rows((own, count), 0, me, rows_local, True) == lax.broadcasted_iota(jnp.int32, (own, count), 1)
    label = label_ref[:own, 0:1]
    grad = logit_gradient(teacher_ref[:own], student_ref[:own], norms, is_row, label)
    shift = jnp.where((me & 1) == 0, -vocab, vocab).astype(jnp.float32)
    other = logit_gradient(away_ref[0], away_ref[1], norms, is_row, label + shift)
    grads = jnp.concatenate((grad, other), axis=1)
    depth = turned_ref.shape[1]
    step = min(512, depth)
    for k in range(0, depth, step):
        heads = jnp.concatenate((turned_ref[:, k : k + step], other_ref[:, k : k + step]), axis=0)
        part = jnp.dot(grads, heads, preferred_element_type=jnp.float32)
        blocks = [part[b * rows_local : (b + 1) * rows_local] for b in range(8)]
        for out, first, second in ((near_keep, 0, 1), (near_send, 2, 3), (far_keep, 4, 6), (far_send, 5, 7)):
            out[:, k : k + step] = jnp.concatenate((blocks[first], blocks[second]), axis=0).astype(out.dtype)


def whole_grad_kernel(rows_local, me_ref, label_ref, stats_ref, teacher_ref, student_ref, head_ref, out_ref, norms_out):
    count, vocab = student_ref.shape
    norms = merged(stats_ref)[0]
    norms_out[...] = norms
    is_row = held_rows((count, count), 0, me_ref[0], rows_local, False) == lax.broadcasted_iota(
        jnp.int32, (count, count), 1
    )
    grad = logit_gradient(teacher_ref[...], student_ref[...], norms, is_row, label_ref[:, 0:1])
    depth = head_ref.shape[0]
    step = min(512, depth)
    for k in range(0, depth, step):
        out_ref[:, k : k + step] = times_transposed(grad, head_ref[k : k + step])


def gradient(me, label, stats, logits, heads, rows_local, tuned):
    count, vocab = logits[0].shape
    depth = heads[0].shape[1 if tuned else 0]
    vmem = pl.BlockSpec(memory_space=pltpu.VMEM)
    if tuned:
        shapes = [jax.ShapeDtypeStruct((2 * rows_local, depth), kind) for kind in (jnp.float32, jnp.bfloat16)] * 2
    else:
        shapes = [jax.ShapeDtypeStruct((count, depth), jnp.float32)]
    shapes.append(jax.ShapeDtypeStruct((2, count), jnp.float32))
    return pl.pallas_call(
        functools.partial(grad_kernel if tuned else whole_grad_kernel, rows_local),
        in_specs=[pl.BlockSpec(memory_space=pltpu.SMEM)] + [vmem] * (2 + len(logits) + len(heads)),
        out_specs=(vmem,) * len(shapes),
        out_shape=tuple(shapes),
        compiler_params=pltpu.CompilerParams(vmem_limit_bytes=VMEM_LIMIT),
        cost_estimate=pl.CostEstimate(
            flops=2 * count * depth * vocab, bytes_accessed=2 * depth * (vocab + 2 * count), transcendentals=2 * count * vocab
        ),
    )(me, label, stats, *logits, *heads)


def head_kernel(rows_local, tuned, me_ref, label_ref, norms_ref, teacher_ref, student_ref, *refs):
    *pieces, out_ref, held, sems = refs
    me = me_ref[0]
    count = student_ref.shape[0]
    lanes = lax.broadcasted_iota(jnp.int32, (count, count), 1)
    is_row = held_rows((count, count), 0, me, rows_local, tuned) == lanes
    norms = norms_ref[...]
    grad = logit_gradient(teacher_ref[...], student_ref[...], norms, is_row, label_ref[:, 0:1])
    steps, step, _ = held.shape
    copies = []
    for k in range(steps):
        first = (steps + k) * step
        rows = jnp.concatenate([piece[:, first : first + step] for piece in pieces], axis=0)
        held[k] = lax.dot_general(rows, grad, (((0,), (0,)), ((), ())), preferred_element_type=jnp.float32).astype(
            jnp.bfloat16
        )
        copies.append(pltpu.make_async_copy(held.at[k], out_ref.at[pl.ds(k * step, step)], sems.at[k]))
        copies[-1].start()
    for copy in copies:
        copy.wait()


def head_gradient(me, label, norms, logits, hidden, depth, rows_local, tuned):
    count, vocab = logits[0].shape
    step = min(256, depth)
    vmem = pl.BlockSpec(memory_space=pltpu.VMEM)
    return pl.pallas_call(
        functools.partial(head_kernel, rows_local, tuned),
        in_specs=[pl.BlockSpec(memory_space=pltpu.SMEM)] + [vmem] * (4 + len(hidden)),
        out_specs=pl.BlockSpec(memory_space=pltpu.HBM),
        out_shape=jax.ShapeDtypeStruct((depth, vocab), jnp.bfloat16),
        scratch_shapes=[
            pltpu.VMEM((depth // step, step, vocab), jnp.bfloat16),
            pltpu.SemaphoreType.DMA((depth // step,)),
        ],
        compiler_params=pltpu.CompilerParams(vmem_limit_bytes=VMEM_LIMIT),
        cost_estimate=pl.CostEstimate(
            flops=2 * count * depth * vocab, bytes_accessed=2 * depth * (vocab + count), transcendentals=2 * count * vocab
        ),
    )(me, label, norms, *logits, *hidden)


def loss_kernel(rows_local, me_ref, stats_ref, loss_out):
    count = stats_ref.shape[2]
    norms, cross, label_logit = merged(stats_ref)
    loss = cross - norms[0:1] + norms[1:2] + CE_WEIGHT * (norms[1:2] - label_logit)
    lanes = lax.broadcasted_iota(jnp.int32, (count, count), 1)
    mine = lax.broadcasted_iota(jnp.int32, (count, count), 0) + me_ref[0] * rows_local == lanes
    by_lane = lax.broadcasted_iota(jnp.int32, (count, count), 0) == lanes
    loss_out[...] = jnp.sum(jnp.where(by_lane, to_column(mine, loss), 0.0), axis=0, keepdims=True)


def row_loss(me, stats, rows_local):
    vmem = pl.BlockSpec(memory_space=pltpu.VMEM)
    return pl.pallas_call(
        functools.partial(loss_kernel, rows_local),
        in_specs=[pl.BlockSpec(memory_space=pltpu.SMEM), vmem],
        out_specs=vmem,
        out_shape=jax.ShapeDtypeStruct((1, stats.shape[2]), jnp.float32),
        compiler_params=pltpu.CompilerParams(vmem_limit_bytes=VMEM_LIMIT),
        cost_estimate=pl.CostEstimate(flops=0, bytes_accessed=stats.size * 4, transcendentals=stats.size // 4),
    )(me, stats)


def swap(value, distance, n):
    return lax.ppermute(value, "dp", [(i, i ^ distance) for i in range(n)])


def after(value, *done):
    return lax.optimization_barrier((value, *done))[0]


def join_kernel(teacher_ref, student_ref, out_ref, sems):
    depth = teacher_ref.shape[1]
    copies = [
        pltpu.make_async_copy(ref, out_ref.at[:, pl.ds(j * depth, depth)], sems.at[j])
        for j, ref in enumerate((teacher_ref, student_ref))
    ]
    for copy in copies:
        copy.start()
    for copy in copies:
        copy.wait()


def join_rows(teacher_rows, student_rows):
    count, depth = teacher_rows.shape
    return pl.pallas_call(
        join_kernel,
        in_specs=[pl.BlockSpec(memory_space=pltpu.HBM)] * 2,
        out_specs=pl.BlockSpec(memory_space=pltpu.VMEM),
        out_shape=jax.ShapeDtypeStruct((count, 2 * depth), teacher_rows.dtype),
        scratch_shapes=[pltpu.SemaphoreType.DMA((2,))],
        compiler_params=pltpu.CompilerParams(vmem_limit_bytes=2**20),
        cost_estimate=pl.CostEstimate(flops=0, bytes_accessed=8 * count * depth, transcendentals=0),
    )(stay(teacher_rows), stay(student_rows))


def gather_rows(teacher_rows, student_rows, n, fetch):
    join = lambda pair: jnp.concatenate(pair, axis=1)
    stack = lambda *parts: jnp.concatenate(parts, axis=0)
    far_teacher = swap(teacher_rows, 8, n)
    rows = join_rows(teacher_rows, student_rows)
    far_student = swap(student_rows, 8, n)
    near, side = swap(rows, 4, n), swap(rows, 2, n)
    *fetched, turned = fetch(rows)
    far = after(join((far_teacher, far_student)), *fetched, turned)
    far_near = swap(far, 4, n)
    other_head = swap(after(turned, far), 1, n)
    far_side = swap(far, 2, n)
    near_side = swap(side, 4, n)
    far_near_side = swap(far_near, 2, n)
    held = [stack(rows, side, near, near_side, far, far_side), stack(far_near, far_near_side)]
    return held + [swap(piece, 1, n) for piece in held], fetched, (turned, other_head)


def scatter_rows(near_keep, near_send, far_keep, far_send, rows_local, n, head_gradient_of, loss_of):
    low = jnp.bfloat16
    full = jnp.float32
    far_other = swap(far_send, 2, n)
    near_other = swap(near_send, 4, n)
    grad_head = head_gradient_of(far_send)
    far = (far_keep + far_other.astype(full)).astype(low)
    from_far = swap(far[:rows_local], 8, n)
    from_far_near = swap(far[rows_local:], 12, n)
    loss = loss_of(far_send)
    near = near_keep + near_other.astype(full)
    from_side = swap(near[rows_local:].astype(low), 2, n)
    total = lax.optimization_barrier(near[:rows_local] + from_far.astype(full) + from_far_near.astype(full))
    total = total + from_side.astype(full)
    return total, grad_head, loss


def per_device(n, teacher_hidden, student_hidden, teacher_head, student_head, labels, order):
    rows_local, depth = student_hidden.shape
    tuned = n == 16 and rows_local == 8
    me = lax.axis_index("dp").astype(jnp.int32).reshape(1)
    heads = (teacher_head, student_head)
    fetch = lambda *done: prepare(after(me, *done), order, labels, heads, rows_local, tuned)
    if tuned:
        hidden, fetched, turned = gather_rows(teacher_hidden, student_hidden, n, fetch)
    else:
        fetched = fetch(me)
        rows = jnp.concatenate([teacher_hidden, student_hidden], axis=1)
        hidden = [lax.all_gather(rows, "dp", axis=0, tiled=True)]
    *heads, pick, label = fetched
    *logit, stats = logits(me, pick, label, hidden, heads, n, rows_local, tuned)
    if tuned:
        stats, away = logit.pop(), swap(stats, 1, n)
    stats = lax.all_to_all(stats, "dp", 0, 0)
    head_gradient_of = lambda *done: head_gradient(
        after(me, *done), label, norms, logit, hidden, depth, rows_local, tuned
    )
    loss_of = lambda *done: row_loss(after(me, *done), stats, rows_local)
    if tuned:
        *parts, norms = gradient(me, label, stats, (*logit, away), turned, rows_local, tuned)
        grad_hidden, grad_head, loss = scatter_rows(*parts, rows_local, n, head_gradient_of, loss_of)
    else:
        part, norms = gradient(me, label, stats, logit, heads[1:], rows_local, tuned)
        grad_head, loss = head_gradient_of(part), loss_of(part)
        grad_hidden = lax.psum_scatter(part, "dp", scatter_dimension=0, tiled=True)
    return (loss[0, :rows_local], grad_hidden, grad_head)


def solution(mesh):
    in_specs = (
        P(("groups", "dp"), None),
        P(("groups", "dp"), None),
        P(None, "dp"),
        P(None, "dp"),
        P("groups"),
        P("groups"),
    )
    out_specs = (P(("groups", "dp")), P(("groups", "dp"), None), P("groups", "dp"))
    return jax.shard_map(
        functools.partial(per_device, mesh.shape["dp"]),
        mesh=mesh,
        in_specs=in_specs,
        out_specs=out_specs,
        check_vma=False,
    )
```
